32 devices in a mesh: tm: 8 (over z, x), head: 4 (over y, core).
Axes of the slice: x: 2, y: 2, z: 4, core: 2. Of those that a mesh axis runs over, the one named last changes fastest.
Arguments:
- video_q: bfloat16 [1024, 3072], P('tm', 'head'), may hold values from -12 to 12
- video_k: bfloat16 [1024, 3072], P('tm', 'head'), may hold values from -9 to 9
- video_v: bfloat16 [1024, 3072], P('tm', 'head'), may hold values from -6 to 6
- captions: bfloat16 [2048, 4096], P(('tm', 'head')), may hold values from -12 to 12
- text_k_weight: bfloat16 [4096, 3072], P(None, 'head'), may hold values from -0.09375 to 0.09375
- text_v_weight: bfloat16 [4096, 3072], P(None, 'head'), may hold values from -0.09375 to 0.09375
- shot_spans: int32 [8, 2], replicated, may hold values from 0 to 1024, as said below
- caption_lens: int32 [8], replicated, may hold values from 1 to 256, 1280 in all
Outputs:
- attended: bfloat16 [1024, 3072], P('tm', 'head')
The draws below stay inside these ranges and needn't reach their ends.
Inputs may be any that keep to these rules, and one draw needn't show every extreme that they name: Shot s holds tokens shot_spans[s, 0] to shot_spans[s, 1] - 1; the shots follow one another without gaps, the first starts at 0, the last ends at 1024, each holds one token or more. Caption slots c < caption_lens[s] of shot s are live.
All inputs are finite; a program needn't handle non-finite values.
Results may differ from the reference program's by a relative error of at most 0.0077.
Values may be sent and summed in bfloat16 or wider, within the bound.
A program may use at most 192 MiB of HBM per device.

```python
import math
import jax
import jax.numpy as jnp
import numpy as np
from jax import lax

HEADS = 24
HD = 128
DT = 4096
CAP = 256
SHOTS = 8
D = 3072
TOKENS = 1024


def draw_video_q(key, part):
    key = jax.random.fold_in(key, 3)
    values = 2.0 * jnp.clip(jax.random.normal(key, (TOKENS, D), jnp.float32), -6.0, 6.0)
    return values.astype(jnp.bfloat16)


def draw_video_k(key, part):
    key = jax.random.fold_in(key, 5)
    values = 1.5 * jnp.clip(jax.random.normal(key, (TOKENS, D), jnp.float32), -6.0, 6.0)
    return values.astype(jnp.bfloat16)


def draw_shot_spans(key, part):
    key = jax.random.fold_in(key, 11)
    cuts = jax.random.permutation(key, TOKENS - 1)[:SHOTS - 1] + 1
    cuts = jnp.sort(cuts).astype(jnp.int32)
    starts = jnp.concatenate([jnp.zeros((1,), jnp.int32), cuts])
    finish = jnp.concatenate([cuts, jnp.full((1,), TOKENS, jnp.int32)])
    return jnp.stack([starts, finish], axis=1).astype(jnp.int32)


def block_scale(key, extent, split, low, largest):
    def one(axis_at, parts):
        heights = jax.random.uniform(jax.random.fold_in(jax.random.fold_in(key, 6), axis_at), (parts,), jnp.float32, low / len(split), largest / len(split))
        return jnp.repeat(jnp.exp(heights), extent[axis_at] // parts).reshape((-1,) + (1,) * (len(extent) - axis_at - 1))

    gain = one(*split[0])
    for cut in split[1:]:
        gain = gain * one(*cut)
    return gain


def profile(count, total, reach, slope):
    weights = [(1 << 20) // math.isqrt(standing ** slope) + 1 for standing in range(2, count + 1)]
    rest, counts = total - reach - (count - 1), [1] * (count - 1)
    while rest > 0:
        free = [i for i in range(count - 1) if counts[i] < reach]
        whole, remaining = sum([weights[i] for i in free]), rest
        for i in free:
            addition = min(reach - counts[i], max(1, remaining * weights[i] // whole), rest)
            counts[i] = counts[i] + addition
            rest = rest - addition
    return np.array([reach] + counts)


def ragged_sizes(key, count, total, bound, lean):
    if count == 2:
        one = jax.random.randint(key, (), max(1, total - bound), min(bound, total - 1) + 1)
        return jnp.stack([one, total - one])
    lengths = jnp.asarray(profile(count, total, bound, lean), jnp.int32)
    twos = (count - 1) // 2
    source_of, sink = lengths[1:1 + 2 * twos:2], lengths[2:2 + 2 * twos:2]
    slack = jnp.minimum(source_of - 1, bound - sink)
    shifted = jax.random.randint(jax.random.fold_in(key, 1), (twos,), 0, 1 << 20) % (slack + 1)
    lengths = lengths.at[1:1 + 2 * twos:2].set(source_of - shifted).at[2:2 + 2 * twos:2].set(sink + shifted)
    return lengths[jax.random.permutation(jax.random.fold_in(key, 2), count)]


def normal_values(rng, dims, deviation, limit, cuts=(), held_as=jnp.bfloat16):
    factor_of = block_scale(rng, dims, cuts, -0.22, 0.18) if cuts else 1.0
    result = jax.random.normal(rng, dims, jnp.float32) * deviation * factor_of
    return jnp.minimum(jnp.maximum(result, -limit), limit).astype(held_as)


def setup_inputs(seed: int = 0) -> dict:
    arg_keys = jax.random.split(jax.random.key(seed), 9)
    return {
        "video_q": draw_video_q(jax.random.fold_in(arg_keys[8], 71), 0),
        "video_k": draw_video_k(jax.random.fold_in(arg_keys[8], 71), 0),
        "video_v": normal_values(arg_keys[2], (TOKENS, D), 1.0, 6.0, ((0, 8), (1, 4))),
        "captions": normal_values(arg_keys[3], (CAP * SHOTS, DT), 2.0, 12.0, ((0, 32),)),
        "text_k_weight": normal_values(arg_keys[4], (DT, D), DT ** -0.5, 0.09375, ((1, 4),)),
        "text_v_weight": normal_values(arg_keys[5], (DT, D), DT ** -0.5, 0.09375, ((1, 4),)),
        "shot_spans": draw_shot_spans(jax.random.fold_in(arg_keys[8], 71), 0),
        "caption_lens": ragged_sizes(arg_keys[7], SHOTS, 5 * CAP, CAP, 2).astype(jnp.int32),
    }


def reference(video_q, video_k, video_v, captions, text_k_weight, text_v_weight, shot_spans, caption_lens):
    text_keys = jnp.dot(captions, text_k_weight, preferred_element_type=jnp.float32).astype(jnp.bfloat16)
    text_values = jnp.dot(captions, text_v_weight, preferred_element_type=jnp.float32).astype(jnp.bfloat16)
    key_rows = jnp.concatenate([video_k, text_keys], axis=0)
    value_rows = jnp.concatenate([video_v, text_values], axis=0)
    position = jnp.arange(TOKENS, dtype=jnp.int32)
    shot_ids = jnp.arange(SHOTS, dtype=jnp.int32)
    inside = (position[:, None] >= shot_spans[None, :, 0]) & (position[:, None] < shot_spans[None, :, 1])
    shot_of = lax.optimization_barrier(jnp.sum(jnp.where(inside, shot_ids[None, :], 0), axis=1)).astype(jnp.int32)
    row_index = jnp.arange(SHOTS * CAP, dtype=jnp.int32)
    row_shot = row_index % SHOTS
    row_pos = row_index // SHOTS
    row_len = caption_lens[row_shot]
    text_allowed = (shot_of[:, None] == row_shot[None, :]) & (row_pos < row_len)[None, :]
    allowed = jnp.concatenate([jnp.ones((TOKENS, TOKENS), dtype=bool), text_allowed], axis=1)
    inv_scale = 1.0 / math.sqrt(HD)

    def one_head(head_index):
        column = (head_index * HD).astype(jnp.int32)
        query_head = lax.dynamic_slice_in_dim(video_q, column, HD, 1)
        key_head = lax.dynamic_slice_in_dim(key_rows, column, HD, 1)
        value_head = lax.dynamic_slice_in_dim(value_rows, column, HD, 1)
        scores = jnp.dot(query_head, key_head.T, preferred_element_type=jnp.float32) * inv_scale
        scores = jnp.where(allowed, scores, -jnp.inf)
        weights = jnp.exp(scores - lax.optimization_barrier(jnp.max(scores, axis=1, keepdims=True)))
        totals = lax.optimization_barrier(jnp.sum(weights, axis=1, keepdims=True))
        mixed = jnp.dot(weights.astype(jnp.bfloat16), value_head, preferred_element_type=jnp.float32)
        return (mixed / totals).astype(jnp.bfloat16)
    per_head = lax.map(one_head, jnp.arange(HEADS, dtype=jnp.int32))
    return jnp.transpose(per_head, (1, 0, 2)).reshape(TOKENS, HEADS * HD)
```

```python
import functools
import math

import jax
import jax.numpy as jnp
from jax import lax
from jax.experimental import pallas as pl
from jax.experimental.pallas import tpu as pltpu
from jax.sharding import PartitionSpec as P

HD = 128
SHOTS = 8


def gathered_form(
    video_q, video_k, video_v, captions, text_k_weight, text_v_weight, shot_spans, caption_lens
):
    tok_rows = video_q.shape[0]
    queries = video_q.reshape(tok_rows, -1, HD)
    heads_here = queries.shape[1]
    inv_scale = 1.0 / math.sqrt(HD)
    offset_tok = lax.axis_index("tm") * tok_rows
    position = offset_tok + jnp.arange(tok_rows, dtype=jnp.int32)
    shot_ids = jnp.arange(SHOTS, dtype=jnp.int32)
    inside = (position[:, None] >= shot_spans[None, :, 0]) & (
        position[:, None] < shot_spans[None, :, 1]
    )
    shot_of = jnp.sum(jnp.where(inside, shot_ids[None, :], 0), axis=1)

    def absorb(running, key_rows, value_rows, allowed):
        run_max, run_sum, run_num = running
        key_heads = key_rows.reshape(key_rows.shape[0], -1, HD)
        value_heads = value_rows.reshape(value_rows.shape[0], -1, HD)
        scores = (
            jnp.einsum("thd,nhd->thn", queries, key_heads, preferred_element_type=jnp.float32)
            * inv_scale
        )
        if allowed is not None:
            scores = jnp.where(allowed[:, None, :], scores, -jnp.inf)
        new_max = jnp.maximum(run_max, jnp.max(scores, axis=2))
        safe_max = jnp.where(new_max == -jnp.inf, 0.0, new_max)
        rescale = jnp.exp(run_max - safe_max)
        weights = jnp.exp(scores - safe_max[:, :, None])
        run_sum = run_sum * rescale + jnp.sum(weights, axis=2)
        run_num = run_num * rescale[:, :, None] + jnp.einsum(
            "thn,nhd->thd",
            weights.astype(jnp.bfloat16),
            value_heads,
            preferred_element_type=jnp.float32,
        )
        return (new_max, run_sum, run_num)

    running = (
        jnp.full((tok_rows, heads_here), -jnp.inf, jnp.float32),
        jnp.zeros((tok_rows, heads_here), jnp.float32),
        jnp.zeros((tok_rows, heads_here, HD), jnp.float32),
    )
    gathered_keys, gathered_values = (
        lax.all_gather(video_k, "tm", axis=0, tiled=True),
        lax.all_gather(video_v, "tm", axis=0, tiled=True),
    )
    running = absorb(running, gathered_keys, gathered_values, None)
    caption_block = lax.all_gather(captions, "head", axis=0, tiled=True)
    text_keys = jnp.dot(caption_block, text_k_weight, preferred_element_type=jnp.float32).astype(
        jnp.bfloat16
    )
    text_values = jnp.dot(caption_block, text_v_weight, preferred_element_type=jnp.float32).astype(
        jnp.bfloat16
    )
    every_key = lax.all_gather(text_keys, "tm", axis=0, tiled=True)
    every_value = lax.all_gather(text_values, "tm", axis=0, tiled=True)
    row_index = jnp.arange(every_key.shape[0], dtype=jnp.int32)
    row_shot = row_index % SHOTS
    row_pos = row_index // SHOTS
    row_len = jnp.sum(
        jnp.where(row_shot[:, None] == shot_ids[None, :], caption_lens[None, :], 0), axis=1
    )
    running = absorb(
        running,
        every_key,
        every_value,
        (shot_of[:, None] == row_shot[None, :]) & (row_pos < row_len)[None, :],
    )
    run_max, run_sum, run_num = running
    return (run_num / run_sum[:, :, None]).astype(jnp.bfloat16).reshape(tok_rows, -1)


ZL = 4
CHUNKS = 4
MESH = pl.DeviceIdType.MESH


def line_order(z, step):
    inner = jnp.where(step == 0, 3, jnp.where(step == 1, 0, jnp.where(step == 2, 2, 1)))
    return jnp.where(z == 0, 3 - step, jnp.where(z == 1, inner, jnp.where(z == 2, 3 - inner, step)))


def merged_kernel(
    q_ref, k_ref, v_ref, cap_ref, wk_hbm, wv_hbm, spans_ref, lens_ref, out_ref,
    q_all, cap_all, w_all, acc, tk, v_t, row_shot, bias,
    part, stat, x_part, x_stat, up_part, up_stat, down_part, down_stat, go_part, go_stat,
    w_sem, own_sem, cap_y_send, cap_y_recv, cap_s_send, cap_s_recv, cap_f_send, cap_f_recv,
    q_recv, q_up_send, q_down_send, q_x_send,
    x_send, x_recv, xs_send, xs_recv,
    z_send, zs_send, up_recv, ups_recv, down_recv, downs_recv,
):
    rows, width = q_ref.shape
    heads = width // HD
    cap_rows = cap_ref.shape[0]
    text_rows = 4 * cap_rows
    depth = cap_ref.shape[1]
    chunk = depth // CHUNKS
    keys = rows + text_rows

    tm = lax.axis_index("tm")
    head = lax.axis_index("head")
    x = lax.rem(tm, 2)
    z = lax.div(tm, 2)
    core = lax.rem(head, 2)
    y = lax.div(head, 2)
    across_x = (tm + 1 - 2 * x, head)
    above = (tm + 2, head)
    below = (tm - 2, head)
    sib_head = head + 1 - 2 * core
    y_head = head + 2 - 4 * y
    far_head = sib_head + 2 - 4 * y
    sibling = (tm, sib_head)
    across_y = (tm, y_head)

    def columns(j):
        return pl.ds(j * chunk, chunk)

    def weight_copies(j):
        return (
            pltpu.make_async_copy(
                wk_hbm.at[columns(j), :], w_all.at[columns(j), pl.ds(0, width)], w_sem.at[0, j]
            ),
            pltpu.make_async_copy(
                wv_hbm.at[columns(j), :], w_all.at[columns(j), pl.ds(width, width)], w_sem.at[1, j]
            ),
        )

    def own_caption(j):
        return pltpu.make_async_copy(
            cap_ref.at[:, columns(j)], cap_all.at[j, head], own_sem.at[j]
        )

    def cap_to_y(j):
        return pltpu.make_async_remote_copy(
            cap_ref.at[:, columns(j)], cap_all.at[j, head], cap_y_send.at[j], cap_y_recv.at[j],
            device_id=across_y, device_id_type=MESH,
        )

    def cap_to_sibling(j):
        return pltpu.make_async_remote_copy(
            cap_ref.at[:, columns(j)], cap_all.at[j, head], cap_s_send.at[j], cap_s_recv.at[j],
            device_id=sibling, device_id_type=MESH,
        )

    def cap_handed_on(j):
        return pltpu.make_async_remote_copy(
            cap_all.at[j, y_head], cap_all.at[j, y_head], cap_f_send.at[j], cap_f_recv.at[j],
            device_id=sibling, device_id_type=MESH,
        )

    def q_copy(source, slot, send, device):
        return pltpu.make_async_remote_copy(
            source, q_all.at[slot], send, q_recv.at[slot], device_id=device, device_id_type=MESH
        )

    barrier = pltpu.get_barrier_semaphore()
    for device in (across_x, sibling, across_y):
        pl.semaphore_signal(barrier, inc=1, device_id=device, device_id_type=MESH)

    @pl.when(z < ZL - 1)
    def _():
        pl.semaphore_signal(barrier, inc=1, device_id=above, device_id_type=MESH)

    @pl.when(z > 0)
    def _():
        pl.semaphore_signal(barrier, inc=1, device_id=below, device_id_type=MESH)

    for j in range(CHUNKS):
        for copy in weight_copies(j):
            copy.start()
        own_caption(j).start()
    q_own = pltpu.make_async_copy(q_ref, q_all.at[tm], own_sem.at[CHUNKS])
    q_own.start()

    pl.semaphore_wait(barrier, jnp.where((z == 0) | (z == ZL - 1), 4, 5))

    for j in range(CHUNKS):
        cap_to_y(j).start()

    @pl.when(z < ZL - 1)
    def _():
        q_copy(q_ref, tm, q_up_send.at[z], above).start()

    @pl.when(z > 0)
    def _():
        q_copy(q_ref, tm, q_down_send.at[z], below).start()

    q_copy(q_ref, tm, q_x_send.at[z], across_x).start()
    for j in range(CHUNKS):
        cap_to_sibling(j).start()

    stat[...] = jnp.ones_like(stat)
    row = lax.broadcasted_iota(jnp.int32, (text_rows, HD), 0)
    shot = row % SHOTS
    slot = (tm * text_rows + row) // SHOTS
    live = jnp.zeros((text_rows, HD), jnp.int32)
    for s in range(SHOTS):
        live = jnp.where(shot == s, lens_ref[s], live)
    row_shot[...] = jnp.where(slot < live, shot, -1)
    for h in range(heads):
        at = slice(h * HD, (h + 1) * HD)
        v_t[at, :rows] = v_ref[:, at].astype(jnp.float32).T.astype(jnp.bfloat16)

    def q_step(k):
        @pl.when(z >= k)
        def _():
            came = tm - 2 * k
            q_copy(q_all.at[came], came, q_up_send.at[z - k], above).wait_recv()

            @pl.when(z < ZL - 1)
            def _():
                q_copy(q_all.at[came], came, q_up_send.at[z - k], above).start()

            q_copy(q_all.at[came], came, q_x_send.at[z - k], across_x).start()

        @pl.when(z + k < ZL)
        def _():
            came = tm + 2 * k
            q_copy(q_all.at[came], came, q_down_send.at[z + k], below).wait_recv()

            @pl.when(z > 0)
            def _():
                q_copy(q_all.at[came], came, q_down_send.at[z + k], below).start()

            q_copy(q_all.at[came], came, q_x_send.at[z + k], across_x).start()

    tile = 256
    tiles = 2 * width // tile

    def hand_on(j):
        cap_to_y(j).wait_recv()
        cap_handed_on(j).start()

    def project(j):
        own_caption(j).wait()
        cap_to_sibling(j).wait_recv()
        cap_handed_on(j).wait_recv()
        for copy in weight_copies(j):
            copy.wait()

        @pl.loop(0, tiles)
        def _(n):
            at = pl.ds(pl.multiple_of(n * tile, tile), tile)
            block = cap_all[j].reshape(text_rows, chunk)
            term = jnp.dot(block, w_all[columns(j), at], preferred_element_type=jnp.float32)
            if j == 0:
                acc[:, at] = term
            else:
                acc[:, at] += term

    hand_on(0)
    q_step(1)
    hand_on(1)
    project(0)
    hand_on(2)
    project(1)
    q_step(2)
    hand_on(3)
    project(2)
    q_step(3)
    project(3)

    tk[...] = acc[:, :width].astype(jnp.bfloat16)
    for h in range(heads):
        v_t[h * HD : (h + 1) * HD, rows:] = (
            acc[:, width + h * HD : width + (h + 1) * HD].T.astype(jnp.bfloat16)
        )

    q_own.wait()
    other_column = tm + 1 - 2 * x - 2 * z

    scale = math.log2(math.e) / math.sqrt(HD)

    def x_copies(to):
        return (
            pltpu.make_async_remote_copy(
                part.at[to, 1 - x], x_part.at[to], x_send.at[to], x_recv.at[to],
                device_id=across_x, device_id_type=MESH,
            ),
            pltpu.make_async_remote_copy(
                stat.at[to, 1 - x], x_stat.at[to], xs_send.at[to], xs_recv.at[to],
                device_id=across_x, device_id_type=MESH,
            ),
        )

    @pl.loop(0, ZL)
    def _(step):
        to = line_order(z, step)
        came = other_column + 2 * to
        q_copy(q_all.at[came], came, q_x_send.at[0], across_x).wait_recv()
        token = to * 2 * rows + lax.broadcasted_iota(jnp.int32, (8, 2 * rows), 1)
        token_shot = jnp.zeros((8, 2 * rows), jnp.int32)
        for s in range(SHOTS):
            inside = (token >= spans_ref[s, 0]) & (token < spans_ref[s, 1])
            token_shot = jnp.where(inside, s, token_shot)
        of_token = token_shot[:1]
        for half in range(2):
            at = slice(half * rows, (half + 1) * rows)
            bias[:, at] = jnp.where(row_shot[...] == of_token[:, at], 0.0, -jnp.inf)
        for h in range(heads):
            at = slice(h * HD, (h + 1) * HD)
            queries = q_all[pl.ds(2 * to, 2), :, at].reshape(2 * rows, HD)
            dims = (((1,), (1,)), ((), ()))
            video = scale * lax.dot_general(
                k_ref[:, at], queries, dims, preferred_element_type=jnp.float32
            )
            text = (
                scale
                * lax.dot_general(tk[:, at], queries, dims, preferred_element_type=jnp.float32)
                + bias[...]
            )
            top = jnp.maximum(
                jnp.max(video, axis=0, keepdims=True), jnp.max(text, axis=0, keepdims=True)
            )
            video = jnp.exp2(video - top)
            text = jnp.exp2(text - top)
            total = jnp.sum(video, axis=0, keepdims=True) + jnp.sum(text, axis=0, keepdims=True)
            mixed = jnp.dot(
                v_t[at, :rows], video.astype(jnp.bfloat16), preferred_element_type=jnp.float32
            ) + jnp.dot(
                v_t[at, rows:], text.astype(jnp.bfloat16), preferred_element_type=jnp.float32
            )
            for half in range(2):
                lanes = slice(half * rows, (half + 1) * rows)
                part[to, half, at, :] = mixed[:, lanes].astype(jnp.bfloat16)
                stat[to, half, h : h + 1, :] = top[:, lanes]
                stat[to, half, 8 + h : 9 + h, :] = total[:, lanes]
        for copy in x_copies(to):
            copy.start()

    def z_copies(to, device, into_part, into_stat, recv, recv_stat):
        return (
            pltpu.make_async_remote_copy(
                go_part.at[to], into_part.at[to], z_send.at[to], recv.at[to],
                device_id=device, device_id_type=MESH,
            ),
            pltpu.make_async_remote_copy(
                go_stat.at[to], into_stat.at[to], zs_send.at[to], recv_stat.at[to],
                device_id=device, device_id_type=MESH,
            ),
        )

    def up_copies(to):
        return z_copies(to, above, up_part, up_stat, up_recv, ups_recv)

    def down_copies(to):
        return z_copies(to, below, down_part, down_stat, down_recv, downs_recv)

    def merge(to, sources, last=False):
        tops = [s[to, 0:8, :] for _, s in sources]
        top = functools.reduce(jnp.maximum, tops)
        factors = [jnp.exp2(t - top) for t in tops]
        total = sum(f * s[to, 8:16, :] for f, (_, s) in zip(factors, sources))
        if last:
            factors = [f / total for f in factors]
        else:
            go_stat[to, 0:8, :] = top
            go_stat[to, 8:16, :] = total
        for h in range(heads):
            at = slice(h * HD, (h + 1) * HD)
            mixed = sum(
                f[h : h + 1, :] * p[to, at, :].astype(jnp.float32)
                for f, (p, _) in zip(factors, sources)
            )
            if last:
                out_ref[:, at] = mixed.T.astype(jnp.bfloat16)
            else:
                go_part[to, at, :] = mixed.astype(jnp.bfloat16)

    own = (part.at[:, x], stat.at[:, x])
    over_x = (x_part, x_stat)
    from_below = (up_part, up_stat)
    from_above = (down_part, down_stat)

    @pl.loop(0, ZL)
    def _(step):
        to = line_order(z, step)
        for copy in x_copies(to):
            copy.wait_recv()

        @pl.when((to >= z) & (z > 0))
        def _():
            for copy in up_copies(to):
                copy.wait_recv()

        @pl.when((to <= z) & (z < ZL - 1))
        def _():
            for copy in down_copies(to):
                copy.wait_recv()

        @pl.when(to > z)
        def _():
            @pl.when(z > 0)
            def _():
                merge(to, [own, over_x, from_below])

            @pl.when(z == 0)
            def _():
                merge(to, [own, over_x])

            for copy in up_copies(to):
                copy.start()

        @pl.when(to < z)
        def _():
            @pl.when(z < ZL - 1)
            def _():
                merge(to, [own, over_x, from_above])

            @pl.when(z == ZL - 1)
            def _():
                merge(to, [own, over_x])

            for copy in down_copies(to):
                copy.start()

        @pl.when(to == z)
        def _():
            @pl.when(z == 0)
            def _():
                merge(to, [own, over_x, from_above], last=True)

            @pl.when(z == ZL - 1)
            def _():
                merge(to, [own, over_x, from_below], last=True)

            @pl.when((z > 0) & (z < ZL - 1))
            def _():
                merge(to, [own, over_x, from_below, from_above], last=True)

    for j in range(CHUNKS):
        cap_to_y(j).wait_send()
        cap_to_sibling(j).wait_send()
        cap_handed_on(j).wait_send()
    for b in range(ZL):
        slot_b = x + 2 * b

        @pl.when((b <= z) & (z < ZL - 1))
        def _():
            q_copy(q_all.at[slot_b], slot_b, q_up_send.at[b], above).wait_send()

        @pl.when((b >= z) & (z > 0))
        def _():
            q_copy(q_all.at[slot_b], slot_b, q_down_send.at[b], below).wait_send()

        q_copy(q_all.at[slot_b], slot_b, q_x_send.at[b], across_x).wait_send()
        for copy in x_copies(b):
            copy.wait_send()

        @pl.when(b > z)
        def _():
            for copy in up_copies(b):
                copy.wait_send()

        @pl.when(b < z)
        def _():
            for copy in down_copies(b):
                copy.wait_send()


def merged_form(
    video_q, video_k, video_v, captions, text_k_weight, text_v_weight, shot_spans, caption_lens
):
    rows, width = video_q.shape
    cap_rows, depth = captions.shape
    text_rows = 4 * cap_rows
    vmem = pl.BlockSpec(memory_space=pltpu.VMEM)
    smem = pl.BlockSpec(memory_space=pltpu.SMEM)
    hbm = pl.BlockSpec(memory_space=pl.ANY)
    bf16, f32 = jnp.bfloat16, jnp.float32
    dma = pltpu.SemaphoreType.DMA
    blocks = pltpu.VMEM((ZL, width, rows), bf16)
    stats = pltpu.VMEM((ZL, 16, rows), f32)
    return pl.pallas_call(
        merged_kernel,
        out_shape=jax.ShapeDtypeStruct((rows, width), bf16),
        in_specs=[vmem, vmem, vmem, vmem, hbm, hbm, smem, smem],
        out_specs=vmem,
        scratch_shapes=[
            pltpu.VMEM((2 * ZL, rows, width), bf16),
            pltpu.VMEM((CHUNKS, 4, cap_rows, depth // CHUNKS), bf16),
            pltpu.VMEM((depth, 2 * width), bf16),
            pltpu.VMEM((text_rows, 2 * width), f32),
            pltpu.VMEM((text_rows, width), bf16),
            pltpu.VMEM((width, rows + text_rows), bf16),
            pltpu.VMEM((text_rows, HD), jnp.int32),
            pltpu.VMEM((text_rows, 2 * rows), f32),
            pltpu.VMEM((ZL, 2, width, rows), bf16),
            pltpu.VMEM((ZL, 2, 16, rows), f32),
            blocks, stats, blocks, stats, blocks, stats, blocks, stats,
            dma((2, CHUNKS)),
            dma((CHUNKS + 1,)),
        ]
        + [dma((CHUNKS,))] * 6
        + [dma((2 * ZL,))]
        + [dma((ZL,))] * 3
        + [dma((ZL,))] * 4
        + [dma((ZL,))] * 6,
        compiler_params=pltpu.CompilerParams(
            collective_id=0, has_side_effects=True, vmem_limit_bytes=48 << 20
        ),
    )(
        video_q, video_k, video_v, captions, text_k_weight, text_v_weight, shot_spans, caption_lens
    )


def solution(mesh):
    placed = (
        P("tm", "head"),
        P("tm", "head"),
        P("tm", "head"),
        P(("tm", "head"), None),
        P(None, "head"),
        P(None, "head"),
        P(),
        P(),
    )
    fits = mesh.shape["tm"] == 2 * ZL and mesh.shape["head"] == 4
    per_device = merged_form if fits else gathered_form
    return jax.shard_map(
        per_device, mesh=mesh, in_specs=placed, out_specs=P("tm", "head"), check_vma=False
    )
```

```python
import functools
import math

import jax
import jax.numpy as jnp
from jax import lax
from jax.experimental import pallas as pl
from jax.experimental.pallas import tpu as pltpu
from jax.sharding import PartitionSpec as P

HD = 128
SHOTS = 8


def gathered_form(
    video_q, video_k, video_v, captions, text_k_weight, text_v_weight, shot_spans, caption_lens
):
    tok_rows = video_q.shape[0]
    queries = video_q.reshape(tok_rows, -1, HD)
    heads_here = queries.shape[1]
    inv_scale = 1.0 / math.sqrt(HD)
    offset_tok = lax.axis_index("tm") * tok_rows
    position = offset_tok + jnp.arange(tok_rows, dtype=jnp.int32)
    shot_ids = jnp.arange(SHOTS, dtype=jnp.int32)
    inside = (position[:, None] >= shot_spans[None, :, 0]) & (
        position[:, None] < shot_spans[None, :, 1]
    )
    shot_of = jnp.sum(jnp.where(inside, shot_ids[None, :], 0), axis=1)

    def absorb(running, key_rows, value_rows, allowed):
        run_max, run_sum, run_num = running
        key_heads = key_rows.reshape(key_rows.shape[0], -1, HD)
        value_heads = value_rows.reshape(value_rows.shape[0], -1, HD)
        scores = (
            jnp.einsum("thd,nhd->thn", queries, key_heads, preferred_element_type=jnp.float32)
            * inv_scale
        )
        if allowed is not None:
            scores = jnp.where(allowed[:, None, :], scores, -jnp.inf)
        new_max = jnp.maximum(run_max, jnp.max(scores, axis=2))
        safe_max = jnp.where(new_max == -jnp.inf, 0.0, new_max)
        rescale = jnp.exp(run_max - safe_max)
        weights = jnp.exp(scores - safe_max[:, :, None])
        run_sum = run_sum * rescale + jnp.sum(weights, axis=2)
        run_num = run_num * rescale[:, :, None] + jnp.einsum(
            "thn,nhd->thd",
            weights.astype(jnp.bfloat16),
            value_heads,
            preferred_element_type=jnp.float32,
        )
        return (new_max, run_sum, run_num)

    running = (
        jnp.full((tok_rows, heads_here), -jnp.inf, jnp.float32),
        jnp.zeros((tok_rows, heads_here), jnp.float32),
        jnp.zeros((tok_rows, heads_here, HD), jnp.float32),
    )
    gathered_keys, gathered_values = (
        lax.all_gather(video_k, "tm", axis=0, tiled=True),
        lax.all_gather(video_v, "tm", axis=0, tiled=True),
    )
    running = absorb(running, gathered_keys, gathered_values, None)
    caption_block = lax.all_gather(captions, "head", axis=0, tiled=True)
    text_keys = jnp.dot(caption_block, text_k_weight, preferred_element_type=jnp.float32).astype(
        jnp.bfloat16
    )
    text_values = jnp.dot(caption_block, text_v_weight, preferred_element_type=jnp.float32).astype(
        jnp.bfloat16
    )
    every_key = lax.all_gather(text_keys, "tm", axis=0, tiled=True)
    every_value = lax.all_gather(text_values, "tm", axis=0, tiled=True)
    row_index = jnp.arange(every_key.shape[0], dtype=jnp.int32)
    row_shot = row_index % SHOTS
    row_pos = row_index // SHOTS
    row_len = jnp.sum(
        jnp.where(row_shot[:, None] == shot_ids[None, :], caption_lens[None, :], 0), axis=1
    )
    running = absorb(
        running,
        every_key,
        every_value,
        (shot_of[:, None] == row_shot[None, :]) & (row_pos < row_len)[None, :],
    )
    run_max, run_sum, run_num = running
    return (run_num / run_sum[:, :, None]).astype(jnp.bfloat16).reshape(tok_rows, -1)


ZL = 4
CHUNKS = 4
MESH = pl.DeviceIdType.MESH


def line_order(z, step):
    inner = jnp.where(step == 0, 3, jnp.where(step == 1, 0, jnp.where(step == 2, 2, 1)))
    return jnp.where(z == 0, 3 - step, jnp.where(z == 1, inner, jnp.where(z == 2, 3 - inner, step)))


def merged_kernel(
    q_ref, k_hbm, v_hbm, cap_ref, wk_hbm, wv_hbm, spans_ref, lens_ref, out_ref,
    k_ref, v_ref,
    q_all, cap_all, w_all, acc, tk, v_t, row_shot, bias,
    part, stat, x_part, x_stat, up_part, up_stat, down_part, down_stat, go_part, go_stat,
    w_sem, own_sem, cap_y_send, cap_y_recv, cap_s_send, cap_s_recv, cap_f_send, cap_f_recv,
    q_recv, q_up_send, q_down_send, q_x_send,
    x_send, x_recv, xs_send, xs_recv,
    z_send, zs_send, up_recv, ups_recv, down_recv, downs_recv,
):
    rows, width = q_ref.shape
    heads = width // HD
    cap_rows = cap_ref.shape[0]
    text_rows = 4 * cap_rows
    depth = cap_ref.shape[1]
    chunk = depth // CHUNKS
    keys = rows + text_rows

    tm = lax.axis_index("tm")
    head = lax.axis_index("head")
    x = lax.rem(tm, 2)
    z = lax.div(tm, 2)
    core = lax.rem(head, 2)
    y = lax.div(head, 2)
    across_x = (tm + 1 - 2 * x, head)
    above = (tm + 2, head)
    below = (tm - 2, head)
    sib_head = head + 1 - 2 * core
    y_head = head + 2 - 4 * y
    far_head = sib_head + 2 - 4 * y
    sibling = (tm, sib_head)
    across_y = (tm, y_head)

    def columns(j):
        return pl.ds(j * chunk, chunk)

    def weight_copies(j):
        return (
            pltpu.make_async_copy(
                wk_hbm.at[columns(j), :], w_all.at[columns(j), pl.ds(0, width)], w_sem.at[0, j]
            ),
            pltpu.make_async_copy(
                wv_hbm.at[columns(j), :], w_all.at[columns(j), pl.ds(width, width)], w_sem.at[1, j]
            ),
        )

    def own_caption(j):
        return pltpu.make_async_copy(
            cap_ref.at[:, columns(j)], cap_all.at[j, head], own_sem.at[j]
        )

    def cap_to_y(j):
        return pltpu.make_async_remote_copy(
            cap_ref.at[:, columns(j)], cap_all.at[j, head], cap_y_send.at[j], cap_y_recv.at[j],
            device_id=across_y, device_id_type=MESH,
        )

    def cap_to_sibling(j):
        return pltpu.make_async_remote_copy(
            cap_ref.at[:, columns(j)], cap_all.at[j, head], cap_s_send.at[j], cap_s_recv.at[j],
            device_id=sibling, device_id_type=MESH,
        )

    def cap_handed_on(j):
        return pltpu.make_async_remote_copy(
            cap_all.at[j, y_head], cap_all.at[j, y_head], cap_f_send.at[j], cap_f_recv.at[j],
            device_id=sibling, device_id_type=MESH,
        )

    def q_copy(source, slot, send, device):
        return pltpu.make_async_remote_copy(
            source, q_all.at[slot], send, q_recv.at[slot], device_id=device, device_id_type=MESH
        )

    barrier = pltpu.get_barrier_semaphore()
    for device in (across_x, sibling, across_y):
        pl.semaphore_signal(barrier, inc=1, device_id=device, device_id_type=MESH)

    @pl.when(z < ZL - 1)
    def _():
        pl.semaphore_signal(barrier, inc=1, device_id=above, device_id_type=MESH)

    @pl.when(z > 0)
    def _():
        pl.semaphore_signal(barrier, inc=1, device_id=below, device_id_type=MESH)

    for j in range(CHUNKS):
        for copy in weight_copies(j):
            copy.start()
        own_caption(j).start()
    q_own = pltpu.make_async_copy(q_ref, q_all.at[tm], own_sem.at[CHUNKS])
    q_own.start()
    k_own = pltpu.make_async_copy(k_hbm, k_ref, own_sem.at[CHUNKS + 1])
    k_own.start()
    v_own = pltpu.make_async_copy(v_hbm, v_ref, own_sem.at[CHUNKS + 2])
    v_own.start()

    pl.semaphore_wait(barrier, jnp.where((z == 0) | (z == ZL - 1), 4, 5))

    for j in range(CHUNKS):
        cap_to_y(j).start()

    @pl.when(z < ZL - 1)
    def _():
        q_copy(q_ref, tm, q_up_send.at[z], above).start()

    @pl.when(z > 0)
    def _():
        q_copy(q_ref, tm, q_down_send.at[z], below).start()

    q_copy(q_ref, tm, q_x_send.at[z], across_x).start()
    for j in range(CHUNKS):
        cap_to_sibling(j).start()

    stat[...] = jnp.ones_like(stat)
    row = lax.broadcasted_iota(jnp.int32, (text_rows, HD), 0)
    shot = row % SHOTS
    slot = (tm * text_rows + row) // SHOTS
    live = jnp.zeros((text_rows, HD), jnp.int32)
    for s in range(SHOTS):
        live = jnp.where(shot == s, lens_ref[s], live)
    row_shot[...] = jnp.where(slot < live, shot, -1)
    v_own.wait()
    for h in range(heads):
        at = slice(h * HD, (h + 1) * HD)
        v_t[at, :rows] = v_ref[:, at].astype(jnp.float32).T.astype(jnp.bfloat16)

    def q_step(k):
        @pl.when(z >= k)
        def _():
            came = tm - 2 * k
            q_copy(q_all.at[came], came, q_up_send.at[z - k], above).wait_recv()

            @pl.when(z < ZL - 1)
            def _():
                q_copy(q_all.at[came], came, q_up_send.at[z - k], above).start()

            q_copy(q_all.at[came], came, q_x_send.at[z - k], across_x).start()

        @pl.when(z + k < ZL)
        def _():
            came = tm + 2 * k
            q_copy(q_all.at[came], came, q_down_send.at[z + k], below).wait_recv()

            @pl.when(z > 0)
            def _():
                q_copy(q_all.at[came], came, q_down_send.at[z + k], below).start()

            q_copy(q_all.at[came], came, q_x_send.at[z + k], across_x).start()

    tile = 256
    tiles = 2 * width // tile

    def hand_on(j):
        cap_to_y(j).wait_recv()
        cap_handed_on(j).start()

    def project(j):
        own_caption(j).wait()
        cap_to_sibling(j).wait_recv()
        cap_handed_on(j).wait_recv()
        for copy in weight_copies(j):
            copy.wait()

        @pl.loop(0, tiles)
        def _(n):
            at = pl.ds(pl.multiple_of(n * tile, tile), tile)
            block = cap_all[j].reshape(text_rows, chunk)
            term = jnp.dot(block, w_all[columns(j), at], preferred_element_type=jnp.float32)
            if j == 0:
                acc[:, at] = term
            else:
                acc[:, at] += term

    hand_on(0)
    q_step(1)
    hand_on(1)
    project(0)
    hand_on(2)
    project(1)
    q_step(2)
    hand_on(3)
    project(2)
    q_step(3)
    project(3)

    tk[...] = acc[:, :width].astype(jnp.bfloat16)
    for h in range(heads):
        v_t[h * HD : (h + 1) * HD, rows:] = (
            acc[:, width + h * HD : width + (h + 1) * HD].T.astype(jnp.bfloat16)
        )

    q_own.wait()
    k_own.wait()
    other_column = tm + 1 - 2 * x - 2 * z

    scale = math.log2(math.e) / math.sqrt(HD)

    def x_copies(to):
        return (
            pltpu.make_async_remote_copy(
                part.at[to, 1 - x], x_part.at[to], x_send.at[to], x_recv.at[to],
                device_id=across_x, device_id_type=MESH,
            ),
            pltpu.make_async_remote_copy(
                stat.at[to, 1 - x], x_stat.at[to], xs_send.at[to], xs_recv.at[to],
                device_id=across_x, device_id_type=MESH,
            ),
        )

    @pl.loop(0, ZL)
    def _(step):
        to = line_order(z, step)
        came = other_column + 2 * to
        q_copy(q_all.at[came], came, q_x_send.at[0], across_x).wait_recv()
        token = to * 2 * rows + lax.broadcasted_iota(jnp.int32, (8, 2 * rows), 1)
        token_shot = jnp.zeros((8, 2 * rows), jnp.int32)
        for s in range(SHOTS):
            inside = (token >= spans_ref[0, s]) & (token < spans_ref[1, s])
            token_shot = jnp.where(inside, s, token_shot)
        of_token = token_shot[:1]
        for half in range(2):
            at = slice(half * rows, (half + 1) * rows)
            bias[:, at] = jnp.where(row_shot[...] == of_token[:, at], 0.0, -jnp.inf)
        for h in range(heads):
            at = slice(h * HD, (h + 1) * HD)
            queries = q_all[pl.ds(2 * to, 2), :, at].reshape(2 * rows, HD)
            dims = (((1,), (1,)), ((), ()))
            video = scale * lax.dot_general(
                k_ref[:, at], queries, dims, preferred_element_type=jnp.float32
            )
            text = (
                scale
                * lax.dot_general(tk[:, at], queries, dims, preferred_element_type=jnp.float32)
                + bias[...]
            )
            top = jnp.maximum(
                jnp.max(video, axis=0, keepdims=True), jnp.max(text, axis=0, keepdims=True)
            )
            video = jnp.exp2(video - top)
            text = jnp.exp2(text - top)
            total = jnp.sum(video, axis=0, keepdims=True) + jnp.sum(text, axis=0, keepdims=True)
            mixed = jnp.dot(
                v_t[at, :rows], video.astype(jnp.bfloat16), preferred_element_type=jnp.float32
            ) + jnp.dot(
                v_t[at, rows:], text.astype(jnp.bfloat16), preferred_element_type=jnp.float32
            )
            for half in range(2):
                lanes = slice(half * rows, (half + 1) * rows)
                part[to, half, at, :] = mixed[:, lanes].astype(jnp.bfloat16)
                stat[to, half, h : h + 1, :] = top[:, lanes]
                stat[to, half, 8 + h : 9 + h, :] = total[:, lanes]
        for copy in x_copies(to):
            copy.start()

    def z_copies(to, device, into_part, into_stat, recv, recv_stat):
        return (
            pltpu.make_async_remote_copy(
                go_part.at[to], into_part.at[to], z_send.at[to], recv.at[to],
                device_id=device, device_id_type=MESH,
            ),
            pltpu.make_async_remote_copy(
                go_stat.at[to], into_stat.at[to], zs_send.at[to], recv_stat.at[to],
                device_id=device, device_id_type=MESH,
            ),
        )

    def up_copies(to):
        return z_copies(to, above, up_part, up_stat, up_recv, ups_recv)

    def down_copies(to):
        return z_copies(to, below, down_part, down_stat, down_recv, downs_recv)

    def merge(to, sources, last=False):
        tops = [s[to, 0:8, :] for _, s in sources]
        top = functools.reduce(jnp.maximum, tops)
        factors = [jnp.exp2(t - top) for t in tops]
        total = sum(f * s[to, 8:16, :] for f, (_, s) in zip(factors, sources))
        if last:
            factors = [f / total for f in factors]
        else:
            go_stat[to, 0:8, :] = top
            go_stat[to, 8:16, :] = total
        for h in range(heads):
            at = slice(h * HD, (h + 1) * HD)
            mixed = sum(
                f[h : h + 1, :] * p[to, at, :].astype(jnp.float32)
                for f, (p, _) in zip(factors, sources)
            )
            if last:
                out_ref[:, at] = mixed.T.astype(jnp.bfloat16)
            else:
                go_part[to, at, :] = mixed.astype(jnp.bfloat16)

    own = (part.at[:, x], stat.at[:, x])
    over_x = (x_part, x_stat)
    from_below = (up_part, up_stat)
    from_above = (down_part, down_stat)

    @pl.loop(0, ZL)
    def _(step):
        to = line_order(z, step)
        for copy in x_copies(to):
            copy.wait_recv()

        @pl.when((to >= z) & (z > 0))
        def _():
            for copy in up_copies(to):
                copy.wait_recv()

        @pl.when((to <= z) & (z < ZL - 1))
        def _():
            for copy in down_copies(to):
                copy.wait_recv()

        @pl.when(to > z)
        def _():
            @pl.when(z > 0)
            def _():
                merge(to, [own, over_x, from_below])

            @pl.when(z == 0)
            def _():
                merge(to, [own, over_x])

            for copy in up_copies(to):
                copy.start()

        @pl.when(to < z)
        def _():
            @pl.when(z < ZL - 1)
            def _():
                merge(to, [own, over_x, from_above])

            @pl.when(z == ZL - 1)
            def _():
                merge(to, [own, over_x])

            for copy in down_copies(to):
                copy.start()

        @pl.when(to == z)
        def _():
            @pl.when(z == 0)
            def _():
                merge(to, [own, over_x, from_above], last=True)

            @pl.when(z == ZL - 1)
            def _():
                merge(to, [own, over_x, from_below], last=True)

            @pl.when((z > 0) & (z < ZL - 1))
            def _():
                merge(to, [own, over_x, from_below, from_above], last=True)

    for j in range(CHUNKS):
        cap_to_y(j).wait_send()
        cap_to_sibling(j).wait_send()
        cap_handed_on(j).wait_send()
    for b in range(ZL):
        slot_b = x + 2 * b

        @pl.when((b <= z) & (z < ZL - 1))
        def _():
            q_copy(q_all.at[slot_b], slot_b, q_up_send.at[b], above).wait_send()

        @pl.when((b >= z) & (z > 0))
        def _():
            q_copy(q_all.at[slot_b], slot_b, q_down_send.at[b], below).wait_send()

        q_copy(q_all.at[slot_b], slot_b, q_x_send.at[b], across_x).wait_send()
        for copy in x_copies(b):
            copy.wait_send()

        @pl.when(b > z)
        def _():
            for copy in up_copies(b):
                copy.wait_send()

        @pl.when(b < z)
        def _():
            for copy in down_copies(b):
                copy.wait_send()


def merged_form(
    video_q, video_k, video_v, captions, text_k_weight, text_v_weight, shot_spans, caption_lens
):
    rows, width = video_q.shape
    cap_rows, depth = captions.shape
    text_rows = 4 * cap_rows
    vmem = pl.BlockSpec(memory_space=pltpu.VMEM)
    smem = pl.BlockSpec(memory_space=pltpu.SMEM)
    hbm = pl.BlockSpec(memory_space=pltpu.HBM)
    bf16, f32 = jnp.bfloat16, jnp.float32
    dma = pltpu.SemaphoreType.DMA
    blocks = pltpu.VMEM((ZL, width, rows), bf16)
    stats = pltpu.VMEM((ZL, 16, rows), f32)
    return pl.pallas_call(
        merged_kernel,
        out_shape=jax.ShapeDtypeStruct((rows, width), bf16),
        in_specs=[hbm, hbm, hbm, hbm, hbm, hbm, smem, smem],
        out_specs=vmem,
        scratch_shapes=[
            pltpu.VMEM((rows, width), bf16),
            pltpu.VMEM((rows, width), bf16),
            pltpu.VMEM((2 * ZL, rows, width), bf16),
            pltpu.VMEM((CHUNKS, 4, cap_rows, depth // CHUNKS), bf16),
            pltpu.VMEM((depth, 2 * width), bf16),
            pltpu.VMEM((text_rows, 2 * width), f32),
            pltpu.VMEM((text_rows, width), bf16),
            pltpu.VMEM((width, rows + text_rows), bf16),
            pltpu.VMEM((text_rows, HD), jnp.int32),
            pltpu.VMEM((text_rows, 2 * rows), f32),
            pltpu.VMEM((ZL, 2, width, rows), bf16),
            pltpu.VMEM((ZL, 2, 16, rows), f32),
            blocks, stats, blocks, stats, blocks, stats, blocks, stats,
            dma((2, CHUNKS)),
            dma((CHUNKS + 3,)),
        ]
        + [dma((CHUNKS,))] * 6
        + [dma((2 * ZL,))]
        + [dma((ZL,))] * 3
        + [dma((ZL,))] * 4
        + [dma((ZL,))] * 6,
        compiler_params=pltpu.CompilerParams(
            collective_id=0, has_side_effects=True, vmem_limit_bytes=63 << 20
        ),
    )(
        video_q, video_k, video_v, captions, text_k_weight, text_v_weight, shot_spans.T, caption_lens
    )


def solution(mesh):
    placed = (
        P("tm", "head"),
        P("tm", "head"),
        P("tm", "head"),
        P(("tm", "head"), None),
        P(None, "head"),
        P(None, "head"),
        P(),
        P(),
    )
    fits = mesh.shape["tm"] == 2 * ZL and mesh.shape["head"] == 4
    per_device = merged_form if fits else gathered_form
    return jax.shard_map(
        per_device, mesh=mesh, in_specs=placed, out_specs=P("tm", "head"), check_vma=False
    )
```

```python
import functools
import math

import jax
import jax.numpy as jnp
from jax import lax
from jax.experimental import pallas as pl
from jax.experimental.pallas import tpu as pltpu
from jax.sharding import PartitionSpec as P

HD = 128
SHOTS = 8


def gathered_form(
    video_q, video_k, video_v, captions, text_k_weight, text_v_weight, shot_spans, caption_lens
):
    tok_rows = video_q.shape[0]
    queries = video_q.reshape(tok_rows, -1, HD)
    heads_here = queries.shape[1]
    inv_scale = 1.0 / math.sqrt(HD)
    offset_tok = lax.axis_index("tm") * tok_rows
    position = offset_tok + jnp.arange(tok_rows, dtype=jnp.int32)
    shot_ids = jnp.arange(SHOTS, dtype=jnp.int32)
    inside = (position[:, None] >= shot_spans[None, :, 0]) & (
        position[:, None] < shot_spans[None, :, 1]
    )
    shot_of = jnp.sum(jnp.where(inside, shot_ids[None, :], 0), axis=1)

    def absorb(running, key_rows, value_rows, allowed):
        run_max, run_sum, run_num = running
        key_heads = key_rows.reshape(key_rows.shape[0], -1, HD)
        value_heads = value_rows.reshape(value_rows.shape[0], -1, HD)
        scores = (
            jnp.einsum("thd,nhd->thn", queries, key_heads, preferred_element_type=jnp.float32)
            * inv_scale
        )
        if allowed is not None:
            scores = jnp.where(allowed[:, None, :], scores, -jnp.inf)
        new_max = jnp.maximum(run_max, jnp.max(scores, axis=2))
        safe_max = jnp.where(new_max == -jnp.inf, 0.0, new_max)
        rescale = jnp.exp(run_max - safe_max)
        weights = jnp.exp(scores - safe_max[:, :, None])
        run_sum = run_sum * rescale + jnp.sum(weights, axis=2)
        run_num = run_num * rescale[:, :, None] + jnp.einsum(
            "thn,nhd->thd",
            weights.astype(jnp.bfloat16),
            value_heads,
            preferred_element_type=jnp.float32,
        )
        return (new_max, run_sum, run_num)

    running = (
        jnp.full((tok_rows, heads_here), -jnp.inf, jnp.float32),
        jnp.zeros((tok_rows, heads_here), jnp.float32),
        jnp.zeros((tok_rows, heads_here, HD), jnp.float32),
    )
    gathered_keys, gathered_values = (
        lax.all_gather(video_k, "tm", axis=0, tiled=True),
        lax.all_gather(video_v, "tm", axis=0, tiled=True),
    )
    running = absorb(running, gathered_keys, gathered_values, None)
    caption_block = lax.all_gather(captions, "head", axis=0, tiled=True)
    text_keys = jnp.dot(caption_block, text_k_weight, preferred_element_type=jnp.float32).astype(
        jnp.bfloat16
    )
    text_values = jnp.dot(caption_block, text_v_weight, preferred_element_type=jnp.float32).astype(
        jnp.bfloat16
    )
    every_key = lax.all_gather(text_keys, "tm", axis=0, tiled=True)
    every_value = lax.all_gather(text_values, "tm", axis=0, tiled=True)
    row_index = jnp.arange(every_key.shape[0], dtype=jnp.int32)
    row_shot = row_index % SHOTS
    row_pos = row_index // SHOTS
    row_len = jnp.sum(
        jnp.where(row_shot[:, None] == shot_ids[None, :], caption_lens[None, :], 0), axis=1
    )
    running = absorb(
        running,
        every_key,
        every_value,
        (shot_of[:, None] == row_shot[None, :]) & (row_pos < row_len)[None, :],
    )
    run_max, run_sum, run_num = running
    return (run_num / run_sum[:, :, None]).astype(jnp.bfloat16).reshape(tok_rows, -1)


ZL = 4
CHUNKS = 4
GROUPS = 2
MESH = pl.DeviceIdType.MESH


def line_order(z, step):
    inner = jnp.where(step == 0, 3, jnp.where(step == 1, 0, jnp.where(step == 2, 2, 1)))
    return jnp.where(z == 0, 3 - step, jnp.where(z == 1, inner, jnp.where(z == 2, 3 - inner, step)))


def merged_kernel(
    q_ref, k_hbm, v_hbm, cap_ref, wk_hbm, wv_hbm, spans_ref, lens_ref, out_ref,
    k_ref, v_ref,
    q_all, cap_all, w_all, acc, tk, v_t, row_shot, bias,
    part, stat, x_part, x_stat, up_part, up_stat, down_part, down_stat, go_part, go_stat,
    w_sem, own_sem, cap_y_send, cap_y_recv, cap_s_send, cap_s_recv, cap_f_send, cap_f_recv,
    q_recv, q_up_send, q_down_send, q_x_send,
    q_half_send, q_half_recv,
    x_send, x_recv, xs_send, xs_recv,
    z_send, zs_send, up_recv, ups_recv, down_recv, downs_recv,
):
    rows, width = q_ref.shape
    heads = width // HD
    cap_rows = cap_ref.shape[0]
    text_rows = 4 * cap_rows
    depth = cap_ref.shape[1]
    chunk = depth // CHUNKS
    keys = rows + text_rows

    tm = lax.axis_index("tm")
    head = lax.axis_index("head")
    x = lax.rem(tm, 2)
    z = lax.div(tm, 2)
    core = lax.rem(head, 2)
    y = lax.div(head, 2)
    across_x = (tm + 1 - 2 * x, head)
    above = (tm + 2, head)
    below = (tm - 2, head)
    sib_head = head + 1 - 2 * core
    y_head = head + 2 - 4 * y
    far_head = sib_head + 2 - 4 * y
    sibling = (tm, sib_head)
    across_y = (tm, y_head)

    def columns(j):
        return pl.ds(j * chunk, chunk)

    def weight_copies(j):
        return (
            pltpu.make_async_copy(
                wk_hbm.at[columns(j), :], w_all.at[columns(j), pl.ds(0, width)], w_sem.at[0, j]
            ),
            pltpu.make_async_copy(
                wv_hbm.at[columns(j), :], w_all.at[columns(j), pl.ds(width, width)], w_sem.at[1, j]
            ),
        )

    def own_caption(j):
        return pltpu.make_async_copy(
            cap_ref.at[:, columns(j)], cap_all.at[j, head], own_sem.at[j]
        )

    def cap_to_y(j):
        return pltpu.make_async_remote_copy(
            cap_ref.at[:, columns(j)], cap_all.at[j, head], cap_y_send.at[j], cap_y_recv.at[j],
            device_id=across_y, device_id_type=MESH,
        )

    def cap_to_sibling(j):
        return pltpu.make_async_remote_copy(
            cap_ref.at[:, columns(j)], cap_all.at[j, head], cap_s_send.at[j], cap_s_recv.at[j],
            device_id=sibling, device_id_type=MESH,
        )

    def cap_handed_on(j):
        return pltpu.make_async_remote_copy(
            cap_all.at[j, y_head], cap_all.at[j, y_head], cap_f_send.at[j], cap_f_recv.at[j],
            device_id=sibling, device_id_type=MESH,
        )

    def q_copy(source, slot, send, device):
        return pltpu.make_async_remote_copy(
            source, q_all.at[slot], send, q_recv.at[slot], device_id=device, device_id_type=MESH
        )

    half_rows = rows // 2
    odd = lax.rem(z, 2)
    partner_z = z + 1 - 2 * odd
    partner = (tm + 2 - 4 * odd, head)

    def q_x_half(slot, b):
        lower = q_all.at[slot, pl.ds(0, half_rows)]
        return pltpu.make_async_remote_copy(
            lower, lower, q_x_send.at[b], q_recv.at[slot], device_id=across_x, device_id_type=MESH
        )

    def q_round(slot):
        upper = q_all.at[slot, pl.ds(half_rows, half_rows)]
        return pltpu.make_async_remote_copy(
            upper, upper, q_half_send.at[0], q_half_recv.at[0],
            device_id=partner, device_id_type=MESH,
        )

    barrier = pltpu.get_barrier_semaphore()
    for device in (across_x, sibling, across_y):
        pl.semaphore_signal(barrier, inc=1, device_id=device, device_id_type=MESH)

    @pl.when(z < ZL - 1)
    def _():
        pl.semaphore_signal(barrier, inc=1, device_id=above, device_id_type=MESH)

    @pl.when(z > 0)
    def _():
        pl.semaphore_signal(barrier, inc=1, device_id=below, device_id_type=MESH)

    for j in range(CHUNKS):
        for copy in weight_copies(j):
            copy.start()
        own_caption(j).start()
    q_own = pltpu.make_async_copy(q_ref, q_all.at[tm], own_sem.at[CHUNKS])
    q_own.start()
    k_own = pltpu.make_async_copy(k_hbm, k_ref, own_sem.at[CHUNKS + 1])
    k_own.start()
    v_own = pltpu.make_async_copy(v_hbm, v_ref, own_sem.at[CHUNKS + 2])
    v_own.start()

    pl.semaphore_wait(barrier, jnp.where((z == 0) | (z == ZL - 1), 4, 5))

    for j in range(CHUNKS):
        cap_to_y(j).start()

    @pl.when(z < ZL - 1)
    def _():
        q_copy(q_ref, tm, q_up_send.at[z], above).start()

    @pl.when(z > 0)
    def _():
        q_copy(q_ref, tm, q_down_send.at[z], below).start()

    q_copy(q_ref, tm, q_x_send.at[z], across_x).start()
    for j in range(CHUNKS):
        cap_to_sibling(j).start()

    stat[...] = jnp.ones_like(stat)
    row = lax.broadcasted_iota(jnp.int32, (text_rows, HD), 0)
    shot = row % SHOTS
    slot = (tm * text_rows + row) // SHOTS
    live = jnp.zeros((text_rows, HD), jnp.int32)
    for s in range(SHOTS):
        live = jnp.where(shot == s, lens_ref[s], live)
    row_shot[...] = jnp.where(slot < live, shot, -1)
    v_own.wait()
    for h in range(heads):
        at = slice(h * HD, (h + 1) * HD)
        v_t[at, :rows] = v_ref[:, at].astype(jnp.float32).T.astype(jnp.bfloat16)

    def q_step(k):
        @pl.when(z >= k)
        def _():
            came = tm - 2 * k
            q_copy(q_all.at[came], came, q_up_send.at[z - k], above).wait_recv()

            @pl.when(z < ZL - 1)
            def _():
                q_copy(q_all.at[came], came, q_up_send.at[z - k], above).start()

            if k == 1:
                @pl.when(odd == 1)
                def _():
                    q_x_half(came, z - k).start()

                @pl.when(jnp.logical_not(odd == 1))
                def _():
                    q_copy(q_all.at[came], came, q_x_send.at[z - k], across_x).start()
            else:
                q_copy(q_all.at[came], came, q_x_send.at[z - k], across_x).start()

        @pl.when(z + k < ZL)
        def _():
            came = tm + 2 * k
            q_copy(q_all.at[came], came, q_down_send.at[z + k], below).wait_recv()

            @pl.when(z > 0)
            def _():
                q_copy(q_all.at[came], came, q_down_send.at[z + k], below).start()

            if k == 1:
                @pl.when(odd == 0)
                def _():
                    q_x_half(came, z + k).start()

                @pl.when(jnp.logical_not(odd == 0))
                def _():
                    q_copy(q_all.at[came], came, q_x_send.at[z + k], across_x).start()
            else:
                q_copy(q_all.at[came], came, q_x_send.at[z + k], across_x).start()

        if k == 1:
            beside = tm + 1 - 2 * x
            q_copy(q_all.at[beside], beside, q_x_send.at[z], across_x).wait_recv()
            q_round(beside).start()

    tile = 256
    tiles = 2 * width // tile

    def hand_on(j):
        cap_to_y(j).wait_recv()
        cap_handed_on(j).start()

    def project(j):
        own_caption(j).wait()
        cap_to_sibling(j).wait_recv()
        cap_handed_on(j).wait_recv()
        for copy in weight_copies(j):
            copy.wait()

        @pl.loop(0, tiles)
        def _(n):
            at = pl.ds(pl.multiple_of(n * tile, tile), tile)
            block = cap_all[j].reshape(text_rows, chunk)
            term = jnp.dot(block, w_all[columns(j), at], preferred_element_type=jnp.float32)
            if j == 0:
                acc[:, at] = term
            else:
                acc[:, at] += term

    hand_on(0)
    q_step(1)
    hand_on(1)
    project(0)
    hand_on(2)
    project(1)
    q_step(2)
    hand_on(3)
    project(2)
    q_step(3)
    project(3)

    tk[...] = acc[:, :width].astype(jnp.bfloat16)
    for h in range(heads):
        v_t[h * HD : (h + 1) * HD, rows:] = (
            acc[:, width + h * HD : width + (h + 1) * HD].T.astype(jnp.bfloat16)
        )

    q_own.wait()
    k_own.wait()
    other_column = tm + 1 - 2 * x - 2 * z

    scale = math.log2(math.e) / math.sqrt(HD)

    group = heads // GROUPS

    def of_group(g):
        return pl.ds(g * group * HD, group * HD)

    def x_copies(to, g):
        return (
            pltpu.make_async_remote_copy(
                part.at[to, 1 - x, of_group(g)], x_part.at[to, of_group(g)],
                x_send.at[to, g], x_recv.at[to, g],
                device_id=across_x, device_id_type=MESH,
            ),
            pltpu.make_async_remote_copy(
                stat.at[to, 1 - x, g], x_stat.at[to, g], xs_send.at[to, g], xs_recv.at[to, g],
                device_id=across_x, device_id_type=MESH,
            ),
        )

    @pl.loop(0, ZL)
    def _(step):
        to = line_order(z, step)
        came = other_column + 2 * to

        @pl.when(to == partner_z)
        def _():
            q_x_half(came, 0).wait_recv()
            q_round(came).wait_recv()

        @pl.when((to != partner_z) & (to != z))
        def _():
            q_copy(q_all.at[came], came, q_x_send.at[0], across_x).wait_recv()

        token = to * 2 * rows + lax.broadcasted_iota(jnp.int32, (8, 2 * rows), 1)
        token_shot = jnp.zeros((8, 2 * rows), jnp.int32)
        for s in range(SHOTS):
            inside = (token >= spans_ref[0, s]) & (token < spans_ref[1, s])
            token_shot = jnp.where(inside, s, token_shot)
        of_token = token_shot[:1]
        for half in range(2):
            at = slice(half * rows, (half + 1) * rows)
            bias[:, at] = jnp.where(row_shot[...] == of_token[:, at], 0.0, -jnp.inf)
        for h in range(heads):
            g, r = h // group, h % group
            at = slice(h * HD, (h + 1) * HD)
            queries = q_all[pl.ds(2 * to, 2), :, at].reshape(2 * rows, HD)
            dims = (((1,), (1,)), ((), ()))
            video = scale * lax.dot_general(
                k_ref[:, at], queries, dims, preferred_element_type=jnp.float32
            )
            text = (
                scale
                * lax.dot_general(tk[:, at], queries, dims, preferred_element_type=jnp.float32)
                + bias[...]
            )
            top = jnp.maximum(
                jnp.max(video, axis=0, keepdims=True), jnp.max(text, axis=0, keepdims=True)
            )
            video = jnp.exp2(video - top)
            text = jnp.exp2(text - top)
            total = jnp.sum(video, axis=0, keepdims=True) + jnp.sum(text, axis=0, keepdims=True)
            mixed = jnp.dot(
                v_t[at, :rows], video.astype(jnp.bfloat16), preferred_element_type=jnp.float32
            ) + jnp.dot(
                v_t[at, rows:], text.astype(jnp.bfloat16), preferred_element_type=jnp.float32
            )
            for half in range(2):
                lanes = slice(half * rows, (half + 1) * rows)
                part[to, half, at, :] = mixed[:, lanes].astype(jnp.bfloat16)
                stat[to, half, g, r : r + 1, :] = top[:, lanes]
                stat[to, half, g, 8 + r : 9 + r, :] = total[:, lanes]
            if r == group - 1:
                for copy in x_copies(to, g):
                    copy.start()

    def z_copies(to, g, device, into_part, into_stat, recv, recv_stat):
        return (
            pltpu.make_async_remote_copy(
                go_part.at[to, of_group(g)], into_part.at[to, of_group(g)],
                z_send.at[to, g], recv.at[to, g],
                device_id=device, device_id_type=MESH,
            ),
            pltpu.make_async_remote_copy(
                go_stat.at[to, g], into_stat.at[to, g], zs_send.at[to, g], recv_stat.at[to, g],
                device_id=device, device_id_type=MESH,
            ),
        )

    def up_copies(to, g):
        return z_copies(to, g, above, up_part, up_stat, up_recv, ups_recv)

    def down_copies(to, g):
        return z_copies(to, g, below, down_part, down_stat, down_recv, downs_recv)

    def merge(to, g, sources, last=False):
        tops = [s[to, g, 0:8, :] for _, s in sources]
        top = functools.reduce(jnp.maximum, tops)
        factors = [jnp.exp2(t - top) for t in tops]
        total = sum(f * s[to, g, 8:16, :] for f, (_, s) in zip(factors, sources))
        if last:
            factors = [f / total for f in factors]
        else:
            go_stat[to, g, 0:8, :] = top
            go_stat[to, g, 8:16, :] = total
        for r in range(group):
            h = g * group + r
            at = slice(h * HD, (h + 1) * HD)
            mixed = sum(
                f[r : r + 1, :] * p[to, at, :].astype(jnp.float32)
                for f, (p, _) in zip(factors, sources)
            )
            if last:
                out_ref[:, at] = mixed.T.astype(jnp.bfloat16)
            else:
                go_part[to, at, :] = mixed.astype(jnp.bfloat16)

    own = (part.at[:, x], stat.at[:, x])
    over_x = (x_part, x_stat)
    from_below = (up_part, up_stat)
    from_above = (down_part, down_stat)

    def merge_step(to, g):
        for copy in x_copies(to, g):
            copy.wait_recv()

        @pl.when((to >= z) & (z > 0))
        def _():
            for copy in up_copies(to, g):
                copy.wait_recv()

        @pl.when((to <= z) & (z < ZL - 1))
        def _():
            for copy in down_copies(to, g):
                copy.wait_recv()

        @pl.when(to > z)
        def _():
            @pl.when(z > 0)
            def _():
                merge(to, g, [own, over_x, from_below])

            @pl.when(z == 0)
            def _():
                merge(to, g, [own, over_x])

            for copy in up_copies(to, g):
                copy.start()

        @pl.when(to < z)
        def _():
            @pl.when(z < ZL - 1)
            def _():
                merge(to, g, [own, over_x, from_above])

            @pl.when(z == ZL - 1)
            def _():
                merge(to, g, [own, over_x])

            for copy in down_copies(to, g):
                copy.start()

        @pl.when(to == z)
        def _():
            @pl.when(z == 0)
            def _():
                merge(to, g, [own, over_x, from_above], last=True)

            @pl.when(z == ZL - 1)
            def _():
                merge(to, g, [own, over_x, from_below], last=True)

            @pl.when((z > 0) & (z < ZL - 1))
            def _():
                merge(to, g, [own, over_x, from_below, from_above], last=True)

    @pl.loop(0, ZL)
    def _(step):
        to = line_order(z, step)
        for g in range(GROUPS):
            merge_step(to, g)

    for j in range(CHUNKS):
        cap_to_y(j).wait_send()
        cap_to_sibling(j).wait_send()
        cap_handed_on(j).wait_send()
    q_round(tm + 1 - 2 * x).wait_send()
    for b in range(ZL):
        slot_b = x + 2 * b

        @pl.when((b <= z) & (z < ZL - 1))
        def _():
            q_copy(q_all.at[slot_b], slot_b, q_up_send.at[b], above).wait_send()

        @pl.when((b >= z) & (z > 0))
        def _():
            q_copy(q_all.at[slot_b], slot_b, q_down_send.at[b], below).wait_send()

        @pl.when(b == partner_z)
        def _():
            q_x_half(slot_b, b).wait_send()

        @pl.when(b != partner_z)
        def _():
            q_copy(q_all.at[slot_b], slot_b, q_x_send.at[b], across_x).wait_send()

        for g in range(GROUPS):
            for copy in x_copies(b, g):
                copy.wait_send()

        @pl.when(b > z)
        def _():
            for g in range(GROUPS):
                for copy in up_copies(b, g):
                    copy.wait_send()

        @pl.when(b < z)
        def _():
            for g in range(GROUPS):
                for copy in down_copies(b, g):
                    copy.wait_send()


def merged_form(
    video_q, video_k, video_v, captions, text_k_weight, text_v_weight, shot_spans, caption_lens
):
    rows, width = video_q.shape
    cap_rows, depth = captions.shape
    text_rows = 4 * cap_rows
    vmem = pl.BlockSpec(memory_space=pltpu.VMEM)
    smem = pl.BlockSpec(memory_space=pltpu.SMEM)
    hbm = pl.BlockSpec(memory_space=pltpu.HBM)
    bf16, f32 = jnp.bfloat16, jnp.float32
    dma = pltpu.SemaphoreType.DMA
    blocks = pltpu.VMEM((ZL, width, rows), bf16)
    stats = pltpu.VMEM((ZL, GROUPS, 16, rows), f32)
    return pl.pallas_call(
        merged_kernel,
        out_shape=jax.ShapeDtypeStruct((rows, width), bf16),
        in_specs=[hbm, hbm, hbm, hbm, hbm, hbm, smem, smem],
        out_specs=vmem,
        scratch_shapes=[
            pltpu.VMEM((rows, width), bf16),
            pltpu.VMEM((rows, width), bf16),
            pltpu.VMEM((2 * ZL, rows, width), bf16),
            pltpu.VMEM((CHUNKS, 4, cap_rows, depth // CHUNKS), bf16),
            pltpu.VMEM((depth, 2 * width), bf16),
            pltpu.VMEM((text_rows, 2 * width), f32),
            pltpu.VMEM((text_rows, width), bf16),
            pltpu.VMEM((width, rows + text_rows), bf16),
            pltpu.VMEM((text_rows, HD), jnp.int32),
            pltpu.VMEM((text_rows, 2 * rows), f32),
            pltpu.VMEM((ZL, 2, width, rows), bf16),
            pltpu.VMEM((ZL, 2, GROUPS, 16, rows), f32),
            blocks, stats, blocks, stats, blocks, stats, blocks, stats,
            dma((2, CHUNKS)),
            dma((CHUNKS + 3,)),
        ]
        + [dma((CHUNKS,))] * 6
        + [dma((2 * ZL,))]
        + [dma((ZL,))] * 3
        + [dma((1,))] * 2
        + [dma((ZL, GROUPS))] * 10,
        compiler_params=pltpu.CompilerParams(
            collective_id=0, has_side_effects=True, vmem_limit_bytes=63 << 20
        ),
    )(
        video_q, video_k, video_v, captions, text_k_weight, text_v_weight, shot_spans.T, caption_lens
    )


def solution(mesh):
    placed = (
        P("tm", "head"),
        P("tm", "head"),
        P("tm", "head"),
        P(("tm", "head"), None),
        P(None, "head"),
        P(None, "head"),
        P(),
        P(),
    )
    fits = mesh.shape["tm"] == 2 * ZL and mesh.shape["head"] == 4
    per_device = merged_form if fits else gathered_form
    return jax.shard_map(
        per_device, mesh=mesh, in_specs=placed, out_specs=P("tm", "head"), check_vma=False
    )
```

```python
import functools
import math

import jax
import jax.numpy as jnp
from jax import lax
from jax.experimental import pallas as pl
from jax.experimental.pallas import tpu as pltpu
from jax.sharding import PartitionSpec as P

HD = 128
SHOTS = 8


def gathered_form(
    video_q, video_k, video_v, captions, text_k_weight, text_v_weight, shot_spans, caption_lens
):
    tok_rows = video_q.shape[0]
    queries = video_q.reshape(tok_rows, -1, HD)
    heads_here = queries.shape[1]
    inv_scale = 1.0 / math.sqrt(HD)
    offset_tok = lax.axis_index("tm") * tok_rows
    position = offset_tok + jnp.arange(tok_rows, dtype=jnp.int32)
    shot_ids = jnp.arange(SHOTS, dtype=jnp.int32)
    inside = (position[:, None] >= shot_spans[None, :, 0]) & (
        position[:, None] < shot_spans[None, :, 1]
    )
    shot_of = jnp.sum(jnp.where(inside, shot_ids[None, :], 0), axis=1)

    def absorb(running, key_rows, value_rows, allowed):
        run_max, run_sum, run_num = running
        key_heads = key_rows.reshape(key_rows.shape[0], -1, HD)
        value_heads = value_rows.reshape(value_rows.shape[0], -1, HD)
        scores = (
            jnp.einsum("thd,nhd->thn", queries, key_heads, preferred_element_type=jnp.float32)
            * inv_scale
        )
        if allowed is not None:
            scores = jnp.where(allowed[:, None, :], scores, -jnp.inf)
        new_max = jnp.maximum(run_max, jnp.max(scores, axis=2))
        safe_max = jnp.where(new_max == -jnp.inf, 0.0, new_max)
        rescale = jnp.exp(run_max - safe_max)
        weights = jnp.exp(scores - safe_max[:, :, None])
        run_sum = run_sum * rescale + jnp.sum(weights, axis=2)
        run_num = run_num * rescale[:, :, None] + jnp.einsum(
            "thn,nhd->thd",
            weights.astype(jnp.bfloat16),
            value_heads,
            preferred_element_type=jnp.float32,
        )
        return (new_max, run_sum, run_num)

    running = (
        jnp.full((tok_rows, heads_here), -jnp.inf, jnp.float32),
        jnp.zeros((tok_rows, heads_here), jnp.float32),
        jnp.zeros((tok_rows, heads_here, HD), jnp.float32),
    )
    gathered_keys, gathered_values = (
        lax.all_gather(video_k, "tm", axis=0, tiled=True),
        lax.all_gather(video_v, "tm", axis=0, tiled=True),
    )
    running = absorb(running, gathered_keys, gathered_values, None)
    caption_block = lax.all_gather(captions, "head", axis=0, tiled=True)
    text_keys = jnp.dot(caption_block, text_k_weight, preferred_element_type=jnp.float32).astype(
        jnp.bfloat16
    )
    text_values = jnp.dot(caption_block, text_v_weight, preferred_element_type=jnp.float32).astype(
        jnp.bfloat16
    )
    every_key = lax.all_gather(text_keys, "tm", axis=0, tiled=True)
    every_value = lax.all_gather(text_values, "tm", axis=0, tiled=True)
    row_index = jnp.arange(every_key.shape[0], dtype=jnp.int32)
    row_shot = row_index % SHOTS
    row_pos = row_index // SHOTS
    row_len = jnp.sum(
        jnp.where(row_shot[:, None] == shot_ids[None, :], caption_lens[None, :], 0), axis=1
    )
    running = absorb(
        running,
        every_key,
        every_value,
        (shot_of[:, None] == row_shot[None, :]) & (row_pos < row_len)[None, :],
    )
    run_max, run_sum, run_num = running
    return (run_num / run_sum[:, :, None]).astype(jnp.bfloat16).reshape(tok_rows, -1)


ZL = 4
CHUNKS = 4
GROUPS = 2
MESH = pl.DeviceIdType.MESH


def line_order(z, step):
    inner = jnp.where(step == 0, 3, jnp.where(step == 1, 0, jnp.where(step == 2, 2, 1)))
    return jnp.where(z == 0, 3 - step, jnp.where(z == 1, inner, jnp.where(z == 2, 3 - inner, step)))


def merged_kernel(
    q_ref, k_hbm, v_hbm, cap_ref, wk_hbm, wv_hbm, spans_ref, lens_ref, out_ref,
    k_ref, v_ref,
    q_all, cap_all, w_all, acc, tk, v_t, row_shot, bias,
    part, stat, x_part, x_stat, up_part, up_stat, down_part, down_stat, go_part, go_stat,
    w_sem, own_sem, cap_y_send, cap_y_recv, cap_s_send, cap_s_recv, cap_f_send, cap_f_recv,
    q_recv, q_up_send, q_down_send, q_x_send,
    q_half_send, q_half_recv,
    x_send, x_recv, xs_send, xs_recv,
    z_send, zs_send, up_recv, ups_recv, down_recv, downs_recv,
):
    rows, width = q_ref.shape
    heads = width // HD
    cap_rows = cap_ref.shape[0]
    text_rows = 4 * cap_rows
    depth = cap_ref.shape[1]
    chunk = depth // CHUNKS
    keys = rows + text_rows

    tm = lax.axis_index("tm")
    head = lax.axis_index("head")
    x = lax.rem(tm, 2)
    z = lax.div(tm, 2)
    core = lax.rem(head, 2)
    y = lax.div(head, 2)
    across_x = (tm + 1 - 2 * x, head)
    above = (tm + 2, head)
    below = (tm - 2, head)
    sib_head = head + 1 - 2 * core
    y_head = head + 2 - 4 * y
    far_head = sib_head + 2 - 4 * y
    sibling = (tm, sib_head)
    across_y = (tm, y_head)

    def columns(j):
        return pl.ds(j * chunk, chunk)

    def weight_copies(j):
        return (
            pltpu.make_async_copy(
                wk_hbm.at[columns(j), :], w_all.at[columns(j), pl.ds(0, width)], w_sem.at[0, j]
            ),
            pltpu.make_async_copy(
                wv_hbm.at[columns(j), :], w_all.at[columns(j), pl.ds(width, width)], w_sem.at[1, j]
            ),
        )

    def own_caption(j):
        return pltpu.make_async_copy(
            cap_ref.at[:, columns(j)], cap_all.at[j, head], own_sem.at[j]
        )

    def cap_to_y(j):
        return pltpu.make_async_remote_copy(
            cap_ref.at[:, columns(j)], cap_all.at[j, head], cap_y_send.at[j], cap_y_recv.at[j],
            device_id=across_y, device_id_type=MESH,
        )

    def cap_to_sibling(j):
        return pltpu.make_async_remote_copy(
            cap_ref.at[:, columns(j)], cap_all.at[j, head], cap_s_send.at[j], cap_s_recv.at[j],
            device_id=sibling, device_id_type=MESH,
        )

    def cap_handed_on(j):
        return pltpu.make_async_remote_copy(
            cap_all.at[j, y_head], cap_all.at[j, y_head], cap_f_send.at[j], cap_f_recv.at[j],
            device_id=sibling, device_id_type=MESH,
        )

    half_rows = rows // 2

    def q_copy(source, slot, u, send, b, device):
        at = pl.ds(u * half_rows, half_rows)
        return pltpu.make_async_remote_copy(
            source.at[at], q_all.at[slot, at], send.at[b, u], q_recv.at[slot, u],
            device_id=device, device_id_type=MESH,
        )

    odd = lax.rem(z, 2)
    partner_z = z + 1 - 2 * odd
    partner = (tm + 2 - 4 * odd, head)

    def q_round(slot):
        upper = q_all.at[slot, pl.ds(half_rows, half_rows)]
        return pltpu.make_async_remote_copy(
            upper, upper, q_half_send.at[0], q_half_recv.at[0],
            device_id=partner, device_id_type=MESH,
        )

    barrier = pltpu.get_barrier_semaphore()
    for device in (across_x, sibling, across_y):
        pl.semaphore_signal(barrier, inc=1, device_id=device, device_id_type=MESH)

    @pl.when(z < ZL - 1)
    def _():
        pl.semaphore_signal(barrier, inc=1, device_id=above, device_id_type=MESH)

    @pl.when(z > 0)
    def _():
        pl.semaphore_signal(barrier, inc=1, device_id=below, device_id_type=MESH)

    for j in range(CHUNKS):
        for copy in weight_copies(j):
            copy.start()
        own_caption(j).start()
    q_own = pltpu.make_async_copy(q_ref, q_all.at[tm], own_sem.at[CHUNKS])
    q_own.start()
    k_own = pltpu.make_async_copy(k_hbm, k_ref, own_sem.at[CHUNKS + 1])
    k_own.start()
    v_own = pltpu.make_async_copy(v_hbm, v_ref, own_sem.at[CHUNKS + 2])
    v_own.start()

    pl.semaphore_wait(barrier, jnp.where((z == 0) | (z == ZL - 1), 4, 5))

    for j in range(CHUNKS):
        cap_to_y(j).start()

    for u in range(2):

        @pl.when(z < ZL - 1)
        def _():
            q_copy(q_ref, tm, u, q_up_send, z, above).start()

        @pl.when(z > 0)
        def _():
            q_copy(q_ref, tm, u, q_down_send, z, below).start()

        q_copy(q_ref, tm, u, q_x_send, z, across_x).start()
    for j in range(CHUNKS):
        cap_to_sibling(j).start()

    stat[...] = jnp.ones_like(stat)
    row = lax.broadcasted_iota(jnp.int32, (text_rows, HD), 0)
    shot = row % SHOTS
    slot = (tm * text_rows + row) // SHOTS
    live = jnp.zeros((text_rows, HD), jnp.int32)
    for s in range(SHOTS):
        live = jnp.where(shot == s, lens_ref[s], live)
    row_shot[...] = jnp.where(slot < live, shot, -1)
    v_own.wait()
    for h in range(heads):
        at = slice(h * HD, (h + 1) * HD)
        v_t[at, :rows] = v_ref[:, at].astype(jnp.float32).T.astype(jnp.bfloat16)

    def q_on(k, u, b, send, onward, more):
        came = x + 2 * b
        arrived = q_copy(q_all.at[came], came, u, send, b, onward)
        arrived.wait_recv()

        @pl.when(more)
        def _():
            arrived.start()

        over = q_copy(q_all.at[came], came, u, q_x_send, b, across_x)
        if u == 1 and k == 1:
            @pl.when(b != partner_z)
            def _():
                over.start()
        else:
            over.start()

    def q_step(k):
        for u in range(2):

            @pl.when(z >= k)
            def _():
                q_on(k, u, z - k, q_up_send, above, z < ZL - 1)

            @pl.when(z + k < ZL)
            def _():
                q_on(k, u, z + k, q_down_send, below, z > 0)

        if k == 1:
            beside = tm + 1 - 2 * x
            for u in range(2):
                q_copy(q_all.at[beside], beside, u, q_x_send, z, across_x).wait_recv()
            q_round(beside).start()

    tile = 256
    tiles = 2 * width // tile

    def hand_on(j):
        cap_to_y(j).wait_recv()
        cap_handed_on(j).start()

    def project(j):
        own_caption(j).wait()
        cap_to_sibling(j).wait_recv()
        cap_handed_on(j).wait_recv()
        for copy in weight_copies(j):
            copy.wait()

        @pl.loop(0, tiles)
        def _(n):
            at = pl.ds(pl.multiple_of(n * tile, tile), tile)
            block = cap_all[j].reshape(text_rows, chunk)
            term = jnp.dot(block, w_all[columns(j), at], preferred_element_type=jnp.float32)
            if j == 0:
                acc[:, at] = term
            else:
                acc[:, at] += term

    hand_on(0)
    q_step(1)
    hand_on(1)
    hand_on(2)
    q_step(2)
    project(0)
    hand_on(3)
    project(1)
    q_step(3)
    project(2)
    project(3)

    tk[...] = acc[:, :width].astype(jnp.bfloat16)
    for h in range(heads):
        v_t[h * HD : (h + 1) * HD, rows:] = (
            acc[:, width + h * HD : width + (h + 1) * HD].T.astype(jnp.bfloat16)
        )

    q_own.wait()
    k_own.wait()
    other_column = tm + 1 - 2 * x - 2 * z

    scale = math.log2(math.e) / math.sqrt(HD)

    group = heads // GROUPS

    def of_group(g):
        return pl.ds(g * group * HD, group * HD)

    def x_copies(to, g):
        return (
            pltpu.make_async_remote_copy(
                part.at[to, 1 - x, of_group(g)], x_part.at[to, of_group(g)],
                x_send.at[to, g], x_recv.at[to, g],
                device_id=across_x, device_id_type=MESH,
            ),
            pltpu.make_async_remote_copy(
                stat.at[to, 1 - x, g], x_stat.at[to, g], xs_send.at[to, g], xs_recv.at[to, g],
                device_id=across_x, device_id_type=MESH,
            ),
        )

    @pl.loop(0, ZL)
    def _(step):
        to = line_order(z, step)
        came = other_column + 2 * to

        @pl.when(to == partner_z)
        def _():
            q_copy(q_all.at[came], came, 0, q_x_send, 0, across_x).wait_recv()
            q_round(came).wait_recv()

        @pl.when((to != partner_z) & (to != z))
        def _():
            for u in range(2):
                q_copy(q_all.at[came], came, u, q_x_send, 0, across_x).wait_recv()

        token = to * 2 * rows + lax.broadcasted_iota(jnp.int32, (8, 2 * rows), 1)
        token_shot = jnp.zeros((8, 2 * rows), jnp.int32)
        for s in range(SHOTS):
            inside = (token >= spans_ref[0, s]) & (token < spans_ref[1, s])
            token_shot = jnp.where(inside, s, token_shot)
        of_token = token_shot[:1]
        for half in range(2):
            at = slice(half * rows, (half + 1) * rows)
            bias[:, at] = jnp.where(row_shot[...] == of_token[:, at], 0.0, -jnp.inf)
        for h in range(heads):
            g, r = h // group, h % group
            at = slice(h * HD, (h + 1) * HD)
            queries = q_all[pl.ds(2 * to, 2), :, at].reshape(2 * rows, HD)
            dims = (((1,), (1,)), ((), ()))
            video = scale * lax.dot_general(
                k_ref[:, at], queries, dims, preferred_element_type=jnp.float32
            )
            text = (
                scale
                * lax.dot_general(tk[:, at], queries, dims, preferred_element_type=jnp.float32)
                + bias[...]
            )
            top = jnp.maximum(
                jnp.max(video, axis=0, keepdims=True), jnp.max(text, axis=0, keepdims=True)
            )
            video = jnp.exp2(video - top)
            text = jnp.exp2(text - top)
            total = jnp.sum(video, axis=0, keepdims=True) + jnp.sum(text, axis=0, keepdims=True)
            mixed = jnp.dot(
                v_t[at, :rows], video.astype(jnp.bfloat16), preferred_element_type=jnp.float32
            ) + jnp.dot(
                v_t[at, rows:], text.astype(jnp.bfloat16), preferred_element_type=jnp.float32
            )
            for half in range(2):
                lanes = slice(half * rows, (half + 1) * rows)
                part[to, half, at, :] = mixed[:, lanes].astype(jnp.bfloat16)
                stat[to, half, g, r : r + 1, :] = top[:, lanes]
                stat[to, half, g, 8 + r : 9 + r, :] = total[:, lanes]
            if r == group - 1:
                for copy in x_copies(to, g):
                    copy.start()

    def z_copies(to, g, device, into_part, into_stat, recv, recv_stat):
        return (
            pltpu.make_async_remote_copy(
                go_part.at[to, of_group(g)], into_part.at[to, of_group(g)],
                z_send.at[to, g], recv.at[to, g],
                device_id=device, device_id_type=MESH,
            ),
            pltpu.make_async_remote_copy(
                go_stat.at[to, g], into_stat.at[to, g], zs_send.at[to, g], recv_stat.at[to, g],
                device_id=device, device_id_type=MESH,
            ),
        )

    def up_copies(to, g):
        return z_copies(to, g, above, up_part, up_stat, up_recv, ups_recv)

    def down_copies(to, g):
        return z_copies(to, g, below, down_part, down_stat, down_recv, downs_recv)

    def merge(to, g, sources, last=False):
        tops = [s[to, g, 0:8, :] for _, s in sources]
        top = functools.reduce(jnp.maximum, tops)
        factors = [jnp.exp2(t - top) for t in tops]
        total = sum(f * s[to, g, 8:16, :] for f, (_, s) in zip(factors, sources))
        if last:
            factors = [f / total for f in factors]
        else:
            go_stat[to, g, 0:8, :] = top
            go_stat[to, g, 8:16, :] = total
        for r in range(group):
            h = g * group + r
            at = slice(h * HD, (h + 1) * HD)
            mixed = sum(
                f[r : r + 1, :] * p[to, at, :].astype(jnp.float32)
                for f, (p, _) in zip(factors, sources)
            )
            if last:
                out_ref[:, at] = mixed.T.astype(jnp.bfloat16)
            else:
                go_part[to, at, :] = mixed.astype(jnp.bfloat16)

    own = (part.at[:, x], stat.at[:, x])
    over_x = (x_part, x_stat)
    from_below = (up_part, up_stat)
    from_above = (down_part, down_stat)

    def merge_step(to, g):
        for copy in x_copies(to, g):
            copy.wait_recv()

        @pl.when((to >= z) & (z > 0))
        def _():
            for copy in up_copies(to, g):
                copy.wait_recv()

        @pl.when((to <= z) & (z < ZL - 1))
        def _():
            for copy in down_copies(to, g):
                copy.wait_recv()

        @pl.when(to > z)
        def _():
            @pl.when(z > 0)
            def _():
                merge(to, g, [own, over_x, from_below])

            @pl.when(z == 0)
            def _():
                merge(to, g, [own, over_x])

            for copy in up_copies(to, g):
                copy.start()

        @pl.when(to < z)
        def _():
            @pl.when(z < ZL - 1)
            def _():
                merge(to, g, [own, over_x, from_above])

            @pl.when(z == ZL - 1)
            def _():
                merge(to, g, [own, over_x])

            for copy in down_copies(to, g):
                copy.start()

        @pl.when(to == z)
        def _():
            @pl.when(z == 0)
            def _():
                merge(to, g, [own, over_x, from_above], last=True)

            @pl.when(z == ZL - 1)
            def _():
                merge(to, g, [own, over_x, from_below], last=True)

            @pl.when((z > 0) & (z < ZL - 1))
            def _():
                merge(to, g, [own, over_x, from_below, from_above], last=True)

    @pl.loop(0, ZL)
    def _(step):
        to = line_order(z, step)
        for g in range(GROUPS):
            merge_step(to, g)

    for j in range(CHUNKS):
        cap_to_y(j).wait_send()
        cap_to_sibling(j).wait_send()
        cap_handed_on(j).wait_send()
    q_round(tm + 1 - 2 * x).wait_send()
    for b in range(ZL):
        slot_b = x + 2 * b

        for u in range(2):

            @pl.when((b <= z) & (z < ZL - 1))
            def _():
                q_copy(q_all.at[slot_b], slot_b, u, q_up_send, b, above).wait_send()

            @pl.when((b >= z) & (z > 0))
            def _():
                q_copy(q_all.at[slot_b], slot_b, u, q_down_send, b, below).wait_send()

        q_copy(q_all.at[slot_b], slot_b, 0, q_x_send, b, across_x).wait_send()

        @pl.when(b != partner_z)
        def _():
            q_copy(q_all.at[slot_b], slot_b, 1, q_x_send, b, across_x).wait_send()

        for g in range(GROUPS):
            for copy in x_copies(b, g):
                copy.wait_send()

        @pl.when(b > z)
        def _():
            for g in range(GROUPS):
                for copy in up_copies(b, g):
                    copy.wait_send()

        @pl.when(b < z)
        def _():
            for g in range(GROUPS):
                for copy in down_copies(b, g):
                    copy.wait_send()


def merged_form(
    video_q, video_k, video_v, captions, text_k_weight, text_v_weight, shot_spans, caption_lens
):
    rows, width = video_q.shape
    cap_rows, depth = captions.shape
    text_rows = 4 * cap_rows
    vmem = pl.BlockSpec(memory_space=pltpu.VMEM)
    smem = pl.BlockSpec(memory_space=pltpu.SMEM)
    hbm = pl.BlockSpec(memory_space=pltpu.HBM)
    bf16, f32 = jnp.bfloat16, jnp.float32
    dma = pltpu.SemaphoreType.DMA
    blocks = pltpu.VMEM((ZL, width, rows), bf16)
    stats = pltpu.VMEM((ZL, GROUPS, 16, rows), f32)
    return pl.pallas_call(
        merged_kernel,
        out_shape=jax.ShapeDtypeStruct((rows, width), bf16),
        in_specs=[hbm, hbm, hbm, hbm, hbm, hbm, smem, smem],
        out_specs=vmem,
        scratch_shapes=[
            pltpu.VMEM((rows, width), bf16),
            pltpu.VMEM((rows, width), bf16),
            pltpu.VMEM((2 * ZL, rows, width), bf16),
            pltpu.VMEM((CHUNKS, 4, cap_rows, depth // CHUNKS), bf16),
            pltpu.VMEM((depth, 2 * width), bf16),
            pltpu.VMEM((text_rows, 2 * width), f32),
            pltpu.VMEM((text_rows, width), bf16),
            pltpu.VMEM((width, rows + text_rows), bf16),
            pltpu.VMEM((text_rows, HD), jnp.int32),
            pltpu.VMEM((text_rows, 2 * rows), f32),
            pltpu.VMEM((ZL, 2, width, rows), bf16),
            pltpu.VMEM((ZL, 2, GROUPS, 16, rows), f32),
            blocks, stats, blocks, stats, blocks, stats, blocks, stats,
            dma((2, CHUNKS)),
            dma((CHUNKS + 3,)),
        ]
        + [dma((CHUNKS,))] * 6
        + [dma((2 * ZL, 2))]
        + [dma((ZL, 2))] * 3
        + [dma((1,))] * 2
        + [dma((ZL, GROUPS))] * 10,
        compiler_params=pltpu.CompilerParams(
            collective_id=0, has_side_effects=True, vmem_limit_bytes=63 << 20
        ),
    )(
        video_q, video_k, video_v, captions, text_k_weight, text_v_weight, shot_spans.T, caption_lens
    )


def solution(mesh):
    placed = (
        P("tm", "head"),
        P("tm", "head"),
        P("tm", "head"),
        P(("tm", "head"), None),
        P(None, "head"),
        P(None, "head"),
        P(),
        P(),
    )
    fits = mesh.shape["tm"] == 2 * ZL and mesh.shape["head"] == 4
    per_device = merged_form if fits else gathered_form
    return jax.shard_map(
        per_device, mesh=mesh, in_specs=placed, out_specs=P("tm", "head"), check_vma=False
    )
```

```python
import functools
import math

import jax
import jax.numpy as jnp
from jax import lax
from jax.experimental import pallas as pl
from jax.experimental.pallas import tpu as pltpu
from jax.sharding import PartitionSpec as P

HD = 128
SHOTS = 8


def gathered_form(
    video_q, video_k, video_v, captions, text_k_weight, text_v_weight, shot_spans, caption_lens
):
    tok_rows = video_q.shape[0]
    queries = video_q.reshape(tok_rows, -1, HD)
    heads_here = queries.shape[1]
    inv_scale = 1.0 / math.sqrt(HD)
    offset_tok = lax.axis_index("tm") * tok_rows
    position = offset_tok + jnp.arange(tok_rows, dtype=jnp.int32)
    shot_ids = jnp.arange(SHOTS, dtype=jnp.int32)
    inside = (position[:, None] >= shot_spans[None, :, 0]) & (
        position[:, None] < shot_spans[None, :, 1]
    )
    shot_of = jnp.sum(jnp.where(inside, shot_ids[None, :], 0), axis=1)

    def absorb(running, key_rows, value_rows, allowed):
        run_max, run_sum, run_num = running
        key_heads = key_rows.reshape(key_rows.shape[0], -1, HD)
        value_heads = value_rows.reshape(value_rows.shape[0], -1, HD)
        scores = (
            jnp.einsum("thd,nhd->thn", queries, key_heads, preferred_element_type=jnp.float32)
            * inv_scale
        )
        if allowed is not None:
            scores = jnp.where(allowed[:, None, :], scores, -jnp.inf)
        new_max = jnp.maximum(run_max, jnp.max(scores, axis=2))
        safe_max = jnp.where(new_max == -jnp.inf, 0.0, new_max)
        rescale = jnp.exp(run_max - safe_max)
        weights = jnp.exp(scores - safe_max[:, :, None])
        run_sum = run_sum * rescale + jnp.sum(weights, axis=2)
        run_num = run_num * rescale[:, :, None] + jnp.einsum(
            "thn,nhd->thd",
            weights.astype(jnp.bfloat16),
            value_heads,
            preferred_element_type=jnp.float32,
        )
        return (new_max, run_sum, run_num)

    running = (
        jnp.full((tok_rows, heads_here), -jnp.inf, jnp.float32),
        jnp.zeros((tok_rows, heads_here), jnp.float32),
        jnp.zeros((tok_rows, heads_here, HD), jnp.float32),
    )
    gathered_keys, gathered_values = (
        lax.all_gather(video_k, "tm", axis=0, tiled=True),
        lax.all_gather(video_v, "tm", axis=0, tiled=True),
    )
    running = absorb(running, gathered_keys, gathered_values, None)
    caption_block = lax.all_gather(captions, "head", axis=0, tiled=True)
    text_keys = jnp.dot(caption_block, text_k_weight, preferred_element_type=jnp.float32).astype(
        jnp.bfloat16
    )
    text_values = jnp.dot(caption_block, text_v_weight, preferred_element_type=jnp.float32).astype(
        jnp.bfloat16
    )
    every_key = lax.all_gather(text_keys, "tm", axis=0, tiled=True)
    every_value = lax.all_gather(text_values, "tm", axis=0, tiled=True)
    row_index = jnp.arange(every_key.shape[0], dtype=jnp.int32)
    row_shot = row_index % SHOTS
    row_pos = row_index // SHOTS
    row_len = jnp.sum(
        jnp.where(row_shot[:, None] == shot_ids[None, :], caption_lens[None, :], 0), axis=1
    )
    running = absorb(
        running,
        every_key,
        every_value,
        (shot_of[:, None] == row_shot[None, :]) & (row_pos < row_len)[None, :],
    )
    run_max, run_sum, run_num = running
    return (run_num / run_sum[:, :, None]).astype(jnp.bfloat16).reshape(tok_rows, -1)


ZL = 4
CHUNKS = 4
GROUPS = 2
MESH = pl.DeviceIdType.MESH


def line_order(z, step):
    inner = jnp.where(step == 0, 3, jnp.where(step == 1, 0, jnp.where(step == 2, 2, 1)))
    return jnp.where(z == 0, 3 - step, jnp.where(z == 1, inner, jnp.where(z == 2, 3 - inner, step)))


def merged_kernel(
    q_ref, k_hbm, v_hbm, cap_ref, wk_hbm, wv_hbm, spans_ref, lens_ref, out_ref,
    k_ref, v_ref,
    q_all, cap_all, w_all, acc, tk, v_t, row_shot, bias,
    part, stat, x_part, x_stat, up_part, up_stat, down_part, down_stat, go_part, go_stat,
    w_sem, own_sem, cap_y_send, cap_y_recv, cap_s_send, cap_s_recv, cap_f_send, cap_f_recv,
    q_recv, q_up_send, q_down_send, q_x_send,
    q_half_send, q_half_recv,
    x_send, x_recv, xs_send, xs_recv,
    z_send, zs_send, up_recv, ups_recv, down_recv, downs_recv,
):
    rows, width = q_ref.shape
    heads = width // HD
    cap_rows = cap_ref.shape[0]
    text_rows = 4 * cap_rows
    depth = cap_ref.shape[1]
    chunk = depth // CHUNKS
    keys = rows + text_rows

    tm = lax.axis_index("tm")
    head = lax.axis_index("head")
    x = lax.rem(tm, 2)
    z = lax.div(tm, 2)
    core = lax.rem(head, 2)
    y = lax.div(head, 2)
    across_x = (tm + 1 - 2 * x, head)
    above = (tm + 2, head)
    below = (tm - 2, head)
    sib_head = head + 1 - 2 * core
    y_head = head + 2 - 4 * y
    far_head = sib_head + 2 - 4 * y
    sibling = (tm, sib_head)
    across_y = (tm, y_head)

    def columns(j):
        return pl.ds(j * chunk, chunk)

    def weight_copies(j):
        return (
            pltpu.make_async_copy(
                wk_hbm.at[columns(j), :], w_all.at[columns(j), pl.ds(0, width)], w_sem.at[0, j]
            ),
            pltpu.make_async_copy(
                wv_hbm.at[columns(j), :], w_all.at[columns(j), pl.ds(width, width)], w_sem.at[1, j]
            ),
        )

    def own_caption(j):
        return pltpu.make_async_copy(
            cap_ref.at[:, columns(j)], cap_all.at[j, head], own_sem.at[j]
        )

    def cap_to_y(j):
        return pltpu.make_async_remote_copy(
            cap_ref.at[:, columns(j)], cap_all.at[j, head], cap_y_send.at[j], cap_y_recv.at[j],
            device_id=across_y, device_id_type=MESH,
        )

    def cap_to_sibling(j):
        return pltpu.make_async_remote_copy(
            cap_ref.at[:, columns(j)], cap_all.at[j, head], cap_s_send.at[j], cap_s_recv.at[j],
            device_id=sibling, device_id_type=MESH,
        )

    def cap_handed_on(j):
        return pltpu.make_async_remote_copy(
            cap_all.at[j, y_head], cap_all.at[j, y_head], cap_f_send.at[j], cap_f_recv.at[j],
            device_id=sibling, device_id_type=MESH,
        )

    half_rows = rows // 2

    def q_copy(source, slot, u, send, b, device):
        at = pl.ds(u * half_rows, half_rows)
        return pltpu.make_async_remote_copy(
            source.at[at], q_all.at[slot, at], send.at[b, u], q_recv.at[slot, u],
            device_id=device, device_id_type=MESH,
        )

    odd = lax.rem(z, 2)
    partner_z = z + 1 - 2 * odd
    partner = (tm + 2 - 4 * odd, head)

    def q_round(slot):
        upper = q_all.at[slot, pl.ds(half_rows, half_rows)]
        return pltpu.make_async_remote_copy(
            upper, upper, q_half_send.at[0], q_half_recv.at[0],
            device_id=partner, device_id_type=MESH,
        )

    barrier = pltpu.get_barrier_semaphore()
    for device in (across_x, sibling, across_y):
        pl.semaphore_signal(barrier, inc=1, device_id=device, device_id_type=MESH)

    @pl.when(z < ZL - 1)
    def _():
        pl.semaphore_signal(barrier, inc=1, device_id=above, device_id_type=MESH)

    @pl.when(z > 0)
    def _():
        pl.semaphore_signal(barrier, inc=1, device_id=below, device_id_type=MESH)

    for j in range(CHUNKS):
        for copy in weight_copies(j):
            copy.start()
        own_caption(j).start()
    q_own = pltpu.make_async_copy(q_ref, q_all.at[tm], own_sem.at[CHUNKS])
    q_own.start()
    k_own = pltpu.make_async_copy(k_hbm, k_ref, own_sem.at[CHUNKS + 1])
    k_own.start()
    v_own = pltpu.make_async_copy(v_hbm, v_ref, own_sem.at[CHUNKS + 2])
    v_own.start()

    pl.semaphore_wait(barrier, jnp.where((z == 0) | (z == ZL - 1), 4, 5))

    for j in range(CHUNKS):
        cap_to_y(j).start()

    for u in range(2):

        @pl.when(z < ZL - 1)
        def _():
            q_copy(q_ref, tm, u, q_up_send, z, above).start()

        @pl.when(z > 0)
        def _():
            q_copy(q_ref, tm, u, q_down_send, z, below).start()

        q_copy(q_ref, tm, u, q_x_send, z, across_x).start()
    for j in range(CHUNKS):
        cap_to_sibling(j).start()

    stat[...] = jnp.ones_like(stat)
    row = lax.broadcasted_iota(jnp.int32, (text_rows, HD), 0)
    shot = row % SHOTS
    slot = (tm * text_rows + row) // SHOTS
    live = jnp.zeros((text_rows, HD), jnp.int32)
    for s in range(SHOTS):
        live = jnp.where(shot == s, lens_ref[s], live)
    row_shot[...] = jnp.where(slot < live, shot, -1)
    v_own.wait()
    for h in range(heads):
        at = slice(h * HD, (h + 1) * HD)
        v_t[at, :rows] = v_ref[:, at].astype(jnp.float32).T.astype(jnp.bfloat16)

    def q_on(k, u, b, send, onward, more):
        came = x + 2 * b
        arrived = q_copy(q_all.at[came], came, u, send, b, onward)
        arrived.wait_recv()

        @pl.when(more)
        def _():
            arrived.start()

        over = q_copy(q_all.at[came], came, u, q_x_send, b, across_x)
        if u == 1 and k == 1:
            @pl.when(b != partner_z)
            def _():
                over.start()
        else:
            over.start()

    def q_step(k):
        for u in range(2):

            @pl.when(z >= k)
            def _():
                q_on(k, u, z - k, q_up_send, above, z < ZL - 1)

            @pl.when(z + k < ZL)
            def _():
                q_on(k, u, z + k, q_down_send, below, z > 0)

        if k == 1:
            beside = tm + 1 - 2 * x
            for u in range(2):
                q_copy(q_all.at[beside], beside, u, q_x_send, z, across_x).wait_recv()
            q_round(beside).start()

    tile = 256
    tiles = 2 * width // tile

    def hand_on(j):
        cap_to_y(j).wait_recv()
        cap_handed_on(j).start()

    def project(j):
        own_caption(j).wait()
        cap_to_sibling(j).wait_recv()
        cap_handed_on(j).wait_recv()
        for copy in weight_copies(j):
            copy.wait()

        @pl.loop(0, tiles)
        def _(n):
            at = pl.ds(pl.multiple_of(n * tile, tile), tile)
            block = cap_all[j].reshape(text_rows, chunk)
            term = jnp.dot(block, w_all[columns(j), at], preferred_element_type=jnp.float32)
            if j == 0:
                acc[:, at] = term
            else:
                acc[:, at] += term

    hand_on(0)
    q_step(1)
    hand_on(1)
    hand_on(2)
    q_step(2)
    project(0)
    hand_on(3)
    project(1)
    q_step(3)
    project(2)
    project(3)

    tk[...] = acc[:, :width].astype(jnp.bfloat16)
    for h in range(heads):
        v_t[h * HD : (h + 1) * HD, rows:] = (
            acc[:, width + h * HD : width + (h + 1) * HD].T.astype(jnp.bfloat16)
        )

    q_own.wait()
    k_own.wait()
    other_column = tm + 1 - 2 * x - 2 * z

    scale = math.log2(math.e) / math.sqrt(HD)

    group = heads // GROUPS

    def of_group(g):
        return pl.ds(g * group * HD, group * HD)

    def x_copies(to, g):
        return (
            pltpu.make_async_remote_copy(
                part.at[to, 1 - x, of_group(g)], x_part.at[to, of_group(g)],
                x_send.at[to, g], x_recv.at[to, g],
                device_id=across_x, device_id_type=MESH,
            ),
            pltpu.make_async_remote_copy(
                stat.at[to, 1 - x, g], x_stat.at[to, g], xs_send.at[to, g], xs_recv.at[to, g],
                device_id=across_x, device_id_type=MESH,
            ),
        )

    def attend(step):
        to = line_order(z, step)
        came = other_column + 2 * to

        @pl.when(to == partner_z)
        def _():
            q_copy(q_all.at[came], came, 0, q_x_send, 0, across_x).wait_recv()
            q_round(came).wait_recv()

        @pl.when((to != partner_z) & (to != z))
        def _():
            for u in range(2):
                q_copy(q_all.at[came], came, u, q_x_send, 0, across_x).wait_recv()

        token = to * 2 * rows + lax.broadcasted_iota(jnp.int32, (8, 2 * rows), 1)
        token_shot = jnp.zeros((8, 2 * rows), jnp.int32)
        for s in range(SHOTS):
            inside = (token >= spans_ref[0, s]) & (token < spans_ref[1, s])
            token_shot = jnp.where(inside, s, token_shot)
        of_token = token_shot[:1]
        for half in range(2):
            at = slice(half * rows, (half + 1) * rows)
            bias[:, at] = jnp.where(row_shot[...] == of_token[:, at], 0.0, -jnp.inf)
        for h in range(heads):
            g, r = h // group, h % group
            at = slice(h * HD, (h + 1) * HD)
            queries = q_all[pl.ds(2 * to, 2), :, at].reshape(2 * rows, HD)
            dims = (((1,), (1,)), ((), ()))
            video = scale * lax.dot_general(
                k_ref[:, at], queries, dims, preferred_element_type=jnp.float32
            )
            text = (
                scale
                * lax.dot_general(tk[:, at], queries, dims, preferred_element_type=jnp.float32)
                + bias[...]
            )
            top = jnp.maximum(
                jnp.max(video, axis=0, keepdims=True), jnp.max(text, axis=0, keepdims=True)
            )
            video = jnp.exp2(video - top)
            text = jnp.exp2(text - top)
            total = jnp.sum(video, axis=0, keepdims=True) + jnp.sum(text, axis=0, keepdims=True)
            mixed = jnp.dot(
                v_t[at, :rows], video.astype(jnp.bfloat16), preferred_element_type=jnp.float32
            ) + jnp.dot(
                v_t[at, rows:], text.astype(jnp.bfloat16), preferred_element_type=jnp.float32
            )
            for half in range(2):
                lanes = slice(half * rows, (half + 1) * rows)
                part[to, half, at, :] = mixed[:, lanes].astype(jnp.bfloat16)
                stat[to, half, g, r : r + 1, :] = top[:, lanes]
                stat[to, half, g, 8 + r : 9 + r, :] = total[:, lanes]
            if r == group - 1:
                for copy in x_copies(to, g):
                    copy.start()

    def z_copies(to, g, device, into_part, into_stat, recv, recv_stat):
        return (
            pltpu.make_async_remote_copy(
                go_part.at[to, of_group(g)], into_part.at[to, of_group(g)],
                z_send.at[to, g], recv.at[to, g],
                device_id=device, device_id_type=MESH,
            ),
            pltpu.make_async_remote_copy(
                go_stat.at[to, g], into_stat.at[to, g], zs_send.at[to, g], recv_stat.at[to, g],
                device_id=device, device_id_type=MESH,
            ),
        )

    def up_copies(to, g):
        return z_copies(to, g, above, up_part, up_stat, up_recv, ups_recv)

    def down_copies(to, g):
        return z_copies(to, g, below, down_part, down_stat, down_recv, downs_recv)

    def merge(to, g, sources, last=False):
        tops = [s[to, g, 0:8, :] for _, s in sources]
        top = functools.reduce(jnp.maximum, tops)
        factors = [jnp.exp2(t - top) for t in tops]
        total = sum(f * s[to, g, 8:16, :] for f, (_, s) in zip(factors, sources))
        if last:
            factors = [f / total for f in factors]
        else:
            go_stat[to, g, 0:8, :] = top
            go_stat[to, g, 8:16, :] = total
        for r in range(group):
            h = g * group + r
            at = slice(h * HD, (h + 1) * HD)
            mixed = sum(
                f[r : r + 1, :] * p[to, at, :].astype(jnp.float32)
                for f, (p, _) in zip(factors, sources)
            )
            if last:
                out_ref[:, at] = mixed.T.astype(jnp.bfloat16)
            else:
                go_part[to, at, :] = mixed.astype(jnp.bfloat16)

    own = (part.at[:, x], stat.at[:, x])
    over_x = (x_part, x_stat)
    from_below = (up_part, up_stat)
    from_above = (down_part, down_stat)

    def merge_step(to, g):
        for copy in x_copies(to, g):
            copy.wait_recv()

        @pl.when((to >= z) & (z > 0))
        def _():
            for copy in up_copies(to, g):
                copy.wait_recv()

        @pl.when((to <= z) & (z < ZL - 1))
        def _():
            for copy in down_copies(to, g):
                copy.wait_recv()

        @pl.when(to > z)
        def _():
            @pl.when(z > 0)
            def _():
                merge(to, g, [own, over_x, from_below])

            @pl.when(z == 0)
            def _():
                merge(to, g, [own, over_x])

            for copy in up_copies(to, g):
                copy.start()

        @pl.when(to < z)
        def _():
            @pl.when(z < ZL - 1)
            def _():
                merge(to, g, [own, over_x, from_above])

            @pl.when(z == ZL - 1)
            def _():
                merge(to, g, [own, over_x])

            for copy in down_copies(to, g):
                copy.start()

        @pl.when(to == z)
        def _():
            @pl.when(z == 0)
            def _():
                merge(to, g, [own, over_x, from_above], last=True)

            @pl.when(z == ZL - 1)
            def _():
                merge(to, g, [own, over_x, from_below], last=True)

            @pl.when((z > 0) & (z < ZL - 1))
            def _():
                merge(to, g, [own, over_x, from_below, from_above], last=True)

    @pl.loop(0, ZL + 1)
    def _(turn):
        @pl.when(turn != 2)
        def _():
            attend(jnp.where(turn < 2, turn, turn - 1))

        @pl.when((turn == 2) | (turn == ZL))
        def _():
            @pl.loop(jnp.where(turn == 2, 0, 1), jnp.where(turn == 2, 1, ZL))
            def _(step):
                to = line_order(z, step)
                for g in range(GROUPS):
                    merge_step(to, g)

    for j in range(CHUNKS):
        cap_to_y(j).wait_send()
        cap_to_sibling(j).wait_send()
        cap_handed_on(j).wait_send()
    q_round(tm + 1 - 2 * x).wait_send()
    for b in range(ZL):
        slot_b = x + 2 * b

        for u in range(2):

            @pl.when((b <= z) & (z < ZL - 1))
            def _():
                q_copy(q_all.at[slot_b], slot_b, u, q_up_send, b, above).wait_send()

            @pl.when((b >= z) & (z > 0))
            def _():
                q_copy(q_all.at[slot_b], slot_b, u, q_down_send, b, below).wait_send()

        q_copy(q_all.at[slot_b], slot_b, 0, q_x_send, b, across_x).wait_send()

        @pl.when(b != partner_z)
        def _():
            q_copy(q_all.at[slot_b], slot_b, 1, q_x_send, b, across_x).wait_send()

        for g in range(GROUPS):
            for copy in x_copies(b, g):
                copy.wait_send()

        @pl.when(b > z)
        def _():
            for g in range(GROUPS):
                for copy in up_copies(b, g):
                    copy.wait_send()

        @pl.when(b < z)
        def _():
            for g in range(GROUPS):
                for copy in down_copies(b, g):
                    copy.wait_send()


def merged_form(
    video_q, video_k, video_v, captions, text_k_weight, text_v_weight, shot_spans, caption_lens
):
    rows, width = video_q.shape
    cap_rows, depth = captions.shape
    text_rows = 4 * cap_rows
    vmem = pl.BlockSpec(memory_space=pltpu.VMEM)
    smem = pl.BlockSpec(memory_space=pltpu.SMEM)
    hbm = pl.BlockSpec(memory_space=pltpu.HBM)
    bf16, f32 = jnp.bfloat16, jnp.float32
    dma = pltpu.SemaphoreType.DMA
    blocks = pltpu.VMEM((ZL, width, rows), bf16)
    stats = pltpu.VMEM((ZL, GROUPS, 16, rows), f32)
    return pl.pallas_call(
        merged_kernel,
        out_shape=jax.ShapeDtypeStruct((rows, width), bf16),
        in_specs=[hbm, hbm, hbm, hbm, hbm, hbm, smem, smem],
        out_specs=vmem,
        scratch_shapes=[
            pltpu.VMEM((rows, width), bf16),
            pltpu.VMEM((rows, width), bf16),
            pltpu.VMEM((2 * ZL, rows, width), bf16),
            pltpu.VMEM((CHUNKS, 4, cap_rows, depth // CHUNKS), bf16),
            pltpu.VMEM((depth, 2 * width), bf16),
            pltpu.VMEM((text_rows, 2 * width), f32),
            pltpu.VMEM((text_rows, width), bf16),
            pltpu.VMEM((width, rows + text_rows), bf16),
            pltpu.VMEM((text_rows, HD), jnp.int32),
            pltpu.VMEM((text_rows, 2 * rows), f32),
            pltpu.VMEM((ZL, 2, width, rows), bf16),
            pltpu.VMEM((ZL, 2, GROUPS, 16, rows), f32),
            blocks, stats, blocks, stats, blocks, stats, blocks, stats,
            dma((2, CHUNKS)),
            dma((CHUNKS + 3,)),
        ]
        + [dma((CHUNKS,))] * 6
        + [dma((2 * ZL, 2))]
        + [dma((ZL, 2))] * 3
        + [dma((1,))] * 2
        + [dma((ZL, GROUPS))] * 10,
        compiler_params=pltpu.CompilerParams(
            collective_id=0, has_side_effects=True, vmem_limit_bytes=63 << 20
        ),
    )(
        video_q, video_k, video_v, captions, text_k_weight, text_v_weight, shot_spans.T, caption_lens
    )


def solution(mesh):
    placed = (
        P("tm", "head"),
        P("tm", "head"),
        P("tm", "head"),
        P(("tm", "head"), None),
        P(None, "head"),
        P(None, "head"),
        P(),
        P(),
    )
    fits = mesh.shape["tm"] == 2 * ZL and mesh.shape["head"] == 4
    per_device = merged_form if fits else gathered_form
    return jax.shard_map(
        per_device, mesh=mesh, in_specs=placed, out_specs=P("tm", "head"), check_vma=False
    )
```
